32 devices in a mesh: group: 2 (over y), member: 4 (over z), tile: 2 (over x), sample: 2 (over core).
Axes of the slice: x: 2, y: 2, z: 4, core: 2. Of those that a mesh axis runs over, the one named last changes fastest.
Arguments:
- latent: bfloat16 [4, 4, 4, 512, 256], P(('group', 'sample'), 'member', None, 'tile'), parts along dimension 0, may hold values from -6 to 6
- observed: float32 [4, 8, 4, 512], P(('group', 'sample'), None, None, 'tile'), parts along dimension 0, may hold values from -6 to 6
- radar_valid: int32 [4, 4, 512], P(('group', 'sample'), None, 'tile'), parts along dimension 0, may hold values 0 or 1
- member_order: int32 [4, 4], P(('group', 'sample'), 'member'), parts along dimension 0, may hold values from 0 to 3, each once within a row
- weight_in: bfloat16 [256, 128], replicated, may hold values from -0.375 to 0.375
- weight_mid: bfloat16 [128, 128], replicated, may hold values from -0.5 to 0.5
- weight_out: bfloat16 [128, 8], replicated, may hold values from -0.5 to 0.5
- gains: float32 [4, 128], replicated, may hold values from 0.1 to 1.9
Outputs:
- pixel_score: float32 [4, 8, 4, 512], P(('group', 'sample'), None, 'member', 'tile'), parts along dimension 0
- grad_in: float32 [512, 128], P('group'), parts along dimension 0
- grad_mid: float32 [256, 128], P('group'), parts along dimension 0
- grad_out: float32 [256, 8], P('group'), parts along dimension 0
- grad_gains: float32 [8, 128], P('group'), parts along dimension 0
The draws below stay inside these ranges and needn't reach their ends.
There are 2 independent parts, one for each index of `group`. The reference program is written for one: setup_inputs(seed, part) draws one part's arguments, and reference() takes and returns one part's arrays. A program takes and returns all parts, laid end to end along the dimension named above; an argument that names none is the same for every part. Nothing has to cross between parts.
Inputs may be any that keep to these rules, and one draw needn't show every extreme that they name: `member_order`: for each sample, each member number appears in exactly one slot.
All inputs are finite; a program needn't handle non-finite values. No bound on the sum of `radar_valid` on one device may be relied on, other than what follows from the above.
Results may differ from the reference program's by a relative error of at most 0.0046.
Values may be sent and summed in bfloat16 or wider, within the bound.
No kernel may reach another device: no remote copies, remote signals or barrier semaphores. Data moves between devices by JAX's collectives and lax.ppermute only.
A program may use at most 64 MiB of HBM per device.

```python
import math
import jax
import jax.numpy as jnp
from jax import lax

D = 256
HID = 128
F = 8
MEMBERS = 4
SAMPLES = 2
ROWS = 4
COLS = 512


def set_ends(entries, key, smallest, top_value):
    longest = entries.shape.index(max(entries.shape))
    spots = []
    for shift in (0, 1):
        where = [jax.random.randint(jax.random.fold_in(key, axis), (), 0, length) for axis, length in enumerate(entries.shape)]
        where[longest] = (where[longest] + shift) % entries.shape[longest]
        spots.append(tuple(where))
    return entries.at[spots[0]].set(smallest).at[spots[1]].set(top_value)


def levels(key, shape, pieces, low, largest):
    def one(dim, blocks):
        heights = jax.random.uniform(jax.random.fold_in(jax.random.fold_in(key, 6), dim), (blocks,), jnp.float32, low / len(pieces), largest / len(pieces))
        return jnp.repeat(jnp.exp(heights), shape[dim] // blocks).reshape((-1,) + (1,) * (len(shape) - dim - 1))

    loudness = one(*pieces[0])
    for cut in pieces[1:]:
        loudness = loudness * one(*cut)
    return loudness


def scatter_about(key, shape, scale, reach, cuts=(), kind=jnp.bfloat16):
    array = jax.random.normal(key, shape, jnp.float32) * scale
    if len(cuts) > 0:
        array = levels(key, shape, cuts, -0.22, 0.18) * array
    return jnp.clip(array, min=-reach, max=reach).astype(kind)


def setup_inputs(seed: int = 0, part: int = 0) -> dict:
    streams_of = jax.random.split(jax.random.key(seed), 9)
    part_splits = jax.random.split(jax.random.fold_in(streams_of[8], part), 9)
    latent = scatter_about(part_splits[0], (SAMPLES, MEMBERS, ROWS, COLS, D), 1.0, 6.0, ((0, 2), (1, 4), (3, 2)))
    observed = scatter_about(part_splits[1], (SAMPLES, F, ROWS, COLS), 1.0, 6.0, ((0, 2), (3, 2)), jnp.float32)
    radar_valid = set_ends((jax.random.randint(part_splits[2], (SAMPLES, ROWS, COLS), 0, 4) < 3).astype(jnp.int32), jax.random.fold_in(part_splits[2], 1), 0, 1)
    member_order = jax.vmap(lambda own: jax.random.permutation(own, MEMBERS))(jax.random.split(part_splits[3], SAMPLES)).reshape((SAMPLES, MEMBERS)).astype(jnp.int32)
    weight_in = scatter_about(streams_of[4], (D, HID), D ** -0.5, 0.375)
    weight_mid = scatter_about(streams_of[5], (HID, HID), HID ** -0.5, 0.5)
    weight_out = scatter_about(streams_of[6], (HID, F), HID ** -0.5, 0.5)
    gains = jnp.clip(1.0 + 0.18 * jax.random.normal(streams_of[7], (MEMBERS, HID), jnp.float32), 0.1, 1.9)
    return dict(latent=latent, observed=observed, radar_valid=radar_valid, member_order=member_order, weight_in=weight_in, weight_mid=weight_mid, weight_out=weight_out, gains=gains)


gelu_coef = 0.7978845608028654
cubic_coef = 0.044715
soft_square = 0.0625

def gelu_pair(values):
    inner = jnp.tanh(gelu_coef * (values + cubic_coef * values * values * values))
    output = 0.5 * values * (1.0 + inner)
    slope_part = 0.5 * (1.0 + inner) + 0.5 * values * (1.0 - inner * inner) * gelu_coef * (1.0 + 3.0 * cubic_coef * values * values)
    return (output, slope_part)

def soft_pair(values):
    magnitude = jnp.sqrt(values * values + soft_square)
    return (magnitude, values / magnitude)

def head_forward(inputs, gain_row, weight_in, weight_mid, weight_out):
    pre_one = jnp.dot(inputs, weight_in, preferred_element_type=jnp.float32)
    act_one, slope_one = gelu_pair(pre_one)
    hidden_one = (act_one * gain_row).astype(jnp.bfloat16)
    pre_two = jnp.dot(hidden_one, weight_mid, preferred_element_type=jnp.float32)
    act_two, slope_two = gelu_pair(pre_two)
    hidden_two = act_two.astype(jnp.bfloat16)
    predicted = lax.dot_general(weight_out, hidden_two, (((0,), (1,)), ((), ())), preferred_element_type=jnp.float32)
    return (act_one, slope_one, hidden_one, slope_two, hidden_two, predicted)

def head_backward(inputs, gain_row, weight_in, weight_mid, weight_out, grad_pred):
    act_one, slope_one, hidden_one, slope_two, hidden_two, predicted = head_forward(inputs, gain_row, weight_in, weight_mid, weight_out)
    grad_out = lax.dot_general(hidden_two, grad_pred, (((0,), (1,)), ((), ())), preferred_element_type=jnp.float32)
    grad_hid_two = lax.dot_general(grad_pred, weight_out, (((0,), (1,)), ((), ())), preferred_element_type=jnp.float32)
    grad_pre_two = (grad_hid_two * slope_two).astype(jnp.bfloat16)
    grad_mid = lax.dot_general(hidden_one, grad_pre_two, (((0,), (0,)), ((), ())), preferred_element_type=jnp.float32)
    grad_hid_one = lax.dot_general(grad_pre_two, weight_mid, (((1,), (1,)), ((), ())), preferred_element_type=jnp.float32)
    grad_gain = lax.optimization_barrier(jnp.sum(grad_hid_one * act_one, axis=0))
    grad_pre_one = (grad_hid_one * gain_row * slope_one).astype(jnp.bfloat16)
    grad_in = lax.dot_general(inputs, grad_pre_one, (((0,), (0,)), ((), ())), preferred_element_type=jnp.float32)
    return (grad_in, grad_mid, grad_out, grad_gain)

def pair_sums(member_pred, ensemble):
    magnitude, slope = soft_pair(member_pred[None] - ensemble)
    return (lax.optimization_barrier(jnp.sum(magnitude, axis=0)), lax.optimization_barrier(jnp.sum(slope, axis=0)))

def reference(latent, observed, radar_valid, member_order, weight_in, weight_mid, weight_out, gains):
    samples, members, row_count, col_count, width = latent.shape
    fields = weight_out.shape[1]
    flat = latent.reshape(samples * members, row_count * col_count, width)
    owners = member_order.reshape(samples * members)
    gain_rows = gains[owners]
    predicted = lax.map(lambda item: head_forward(item[0], item[1], weight_in, weight_mid, weight_out)[5], (flat, gain_rows))
    ensemble = predicted.reshape(samples, members, fields, row_count, col_count).transpose(1, 0, 2, 3, 4)
    spread, slopes = lax.map(lambda member: pair_sums(ensemble[member], ensemble), jnp.arange(members, dtype=jnp.int32))
    is_valid = radar_valid.astype(jnp.float32)[:, None]
    skill_mag, skill_slope = soft_pair(ensemble - observed[None])
    skill = lax.optimization_barrier(jnp.sum(skill_mag, axis=0)) / members
    pair_norm = 2.0 * members * (members - 1)
    pixel_score = is_valid * (skill - lax.optimization_barrier(jnp.sum(spread, axis=0)) / pair_norm)
    norm_factor = 1.0 / math.sqrt(samples * row_count * col_count)
    grad_pred = norm_factor * is_valid[None] * (skill_slope / members - slopes / (members * (members - 1.0)))
    grad_pred = grad_pred.astype(jnp.bfloat16).transpose(1, 0, 2, 3, 4).reshape(samples * members, fields, row_count * col_count)
    parts = lax.map(lambda item: head_backward(item[0], item[1], weight_in, weight_mid, weight_out, item[2]), (flat, gain_rows, grad_pred))
    grad_in = lax.optimization_barrier(jnp.sum(parts[0], axis=0))
    grad_mid = lax.optimization_barrier(jnp.sum(parts[1], axis=0))
    grad_out = lax.optimization_barrier(jnp.sum(parts[2], axis=0))
    selector = (owners[:, None] == jnp.arange(members, dtype=jnp.int32)[None, :]).astype(jnp.float32)
    grad_gains = jnp.dot(selector.T, parts[3], precision=lax.Precision.HIGHEST)
    return (pixel_score, grad_in, grad_mid, grad_out, grad_gains)
```

```python
import math

import jax
import jax.numpy as jnp
from jax import lax
from jax.sharding import PartitionSpec as P

gelu_coef = 0.7978845608028654
cubic_coef = 0.044715
soft_square = 0.0625
mesh_axes = ("member", "tile", "sample")


def gelu_pair(values):
    inner = jnp.tanh(gelu_coef * (values + cubic_coef * values * values * values))
    output = 0.5 * values * (1.0 + inner)
    slope_part = 0.5 * (1.0 + inner) + 0.5 * values * (1.0 - inner * inner) * gelu_coef * (
        1.0 + 3.0 * cubic_coef * values * values
    )
    return (output, slope_part)


def soft_pair(values):
    magnitude = jnp.sqrt(values * values + soft_square)
    return (magnitude, values / magnitude)


def swap(array, offset):
    count = 1
    for axis in mesh_axes:
        count *= lax.axis_size(axis)
    return lax.ppermute(array, mesh_axes, [(place, place ^ offset) for place in range(count)])


def rounds_of(bits):
    return [bits[first : first + 2] for first in range(0, len(bits), 2)]


def bits_of(size, lowest):
    assert size & (size - 1) == 0
    return [lowest << place for place in range(size.bit_length() - 1)]


def gather_members(block):
    unit = lax.axis_size("tile") * lax.axis_size("sample")
    stack = [block]
    for bits in rounds_of(bits_of(lax.axis_size("member"), unit)):
        whole = jnp.stack(stack)
        offsets = bits if len(bits) == 1 else [bits[0], bits[1], bits[0] ^ bits[1]]
        arrived = [swap(whole, offset) for offset in offsets]
        stack = stack + [part[k] for part in arrived for k in range(len(stack))]
    return stack


def sum_parameters(rows, link_dtype):
    half = rows.shape[0] // 2
    tiles, samples = lax.axis_size("tile"), lax.axis_size("sample")
    bits = bits_of(tiles, samples) + bits_of(lax.axis_size("member"), samples * tiles)
    place = lax.axis_index(mesh_axes)
    which = place & 1
    for bit in bits:
        which = which ^ jnp.where(place & bit, 1, 0)
    keep = lax.dynamic_slice_in_dim(rows, which * half, half)
    away = lax.dynamic_slice_in_dim(rows, (1 - which) * half, half)
    total = keep + swap(away, 1)
    for group in rounds_of(bits):
        sent = total.astype(link_dtype)
        if len(group) == 1:
            arrived = swap(sent, group[0] ^ 1)
            total = sent.astype(jnp.float32) + arrived.astype(jnp.float32)
        else:
            near, far = group
            parts = [swap(sent, near ^ 1), swap(sent, far ^ 1), swap(sent, near ^ far)]
            parts = [part.astype(jnp.float32) for part in parts]
            total = (sent.astype(jnp.float32) + parts[0]) + (parts[1] + parts[2])
    other = swap(total, 1)
    first = jnp.where(which == 0, total, other)
    second = jnp.where(which == 0, other, total)
    return jnp.concatenate([first, second], axis=0)


def on_device(
    latent, observed, radar_valid, member_order, weight_in, weight_mid, weight_out, gains
):
    row_count = latent.shape[2]
    tile_cols = latent.shape[3]
    width = latent.shape[4]
    fields = weight_out.shape[1]
    hidden = weight_mid.shape[0]
    members = lax.axis_size("member")
    col_count = tile_cols * lax.axis_size("tile")
    norm_factor = 1.0 / math.sqrt(lax.axis_size("sample") * row_count * col_count)
    pair_norm = 2.0 * members * (members - 1)
    selector = (jnp.arange(members, dtype=jnp.int32) == member_order[0, 0]).astype(jnp.float32)
    gain_row = jnp.sum(selector[:, None] * gains, axis=0)
    inputs = latent[0, 0].reshape(row_count * tile_cols, width)
    pre_one = jnp.dot(inputs, weight_in, preferred_element_type=jnp.float32)
    act_one, slope_one = gelu_pair(pre_one)
    hidden_one = (act_one * gain_row).astype(jnp.bfloat16)
    pre_two = jnp.dot(hidden_one, weight_mid, preferred_element_type=jnp.float32)
    act_two, slope_two = gelu_pair(pre_two)
    hidden_two = act_two.astype(jnp.bfloat16)
    predicted = lax.dot_general(
        weight_out, hidden_two, (((0,), (1,)), ((), ())), preferred_element_type=jnp.float32
    )
    mine = predicted.reshape(fields, row_count, tile_cols)
    ensemble = gather_members(mine.astype(jnp.bfloat16))
    others = jnp.stack([part.astype(jnp.float32) for part in ensemble[1:]])
    target = observed[0]
    is_valid = radar_valid[0].astype(jnp.float32)[None]
    own_slope = soft_pair(mine - target)[1]
    slopes = jnp.sum(soft_pair(mine[None] - others)[1], axis=0)
    grad_pred = (
        norm_factor * is_valid * (own_slope / members - slopes / (members * (members - 1.0)))
    )
    grad_pred = grad_pred.astype(jnp.bfloat16)

    own_rows = row_count // members
    first_row = lax.axis_index("member") * own_rows
    row_all = lax.dynamic_slice_in_dim(
        jnp.concatenate([mine[None], others]), first_row, own_rows, axis=2
    )
    row_target = lax.dynamic_slice_in_dim(target, first_row, own_rows, axis=1)
    row_valid = lax.dynamic_slice_in_dim(is_valid, first_row, own_rows, axis=1)
    skill = jnp.sum(soft_pair(row_all - row_target[None])[0], axis=0)
    spread = jnp.sum(soft_pair(row_all[:, None] - row_all[None])[0], axis=(0, 1))
    pixel_score = (row_valid * (skill / members - spread / pair_norm))[None]

    grad_flat = grad_pred.reshape(fields, row_count * tile_cols)
    grad_out = lax.dot_general(
        grad_flat, hidden_two, (((1,), (0,)), ((), ())), preferred_element_type=jnp.float32
    )
    grad_hid_two = lax.dot_general(
        grad_flat, weight_out, (((0,), (1,)), ((), ())), preferred_element_type=jnp.float32
    )
    grad_pre_two = (grad_hid_two * slope_two).astype(jnp.bfloat16)
    grad_mid = lax.dot_general(
        hidden_one, grad_pre_two, (((0,), (0,)), ((), ())), preferred_element_type=jnp.float32
    )
    grad_hid_one = lax.dot_general(
        grad_pre_two, weight_mid, (((1,), (1,)), ((), ())), preferred_element_type=jnp.float32
    )
    grad_gain_row = jnp.sum(grad_hid_one * act_one, axis=0)
    grad_pre_one = (grad_hid_one * gain_row * slope_one).astype(jnp.bfloat16)
    grad_in = lax.dot_general(
        inputs, grad_pre_one, (((0,), (0,)), ((), ())), preferred_element_type=jnp.float32
    )
    grad_gains = selector[:, None] * grad_gain_row[None, :]

    used = width + hidden + fields + members
    padded = -(-used // 32) * 32
    rows = jnp.concatenate(
        [grad_in, grad_mid, grad_out, grad_gains, jnp.zeros((padded - used, hidden), jnp.float32)]
    )
    rows = sum_parameters(rows, jnp.bfloat16)
    cuts = [width, width + hidden, width + hidden + fields, used]
    return (
        pixel_score,
        rows[: cuts[0]],
        rows[cuts[0] : cuts[1]],
        rows[cuts[1] : cuts[2]].T,
        rows[cuts[2] : cuts[3]],
    )


def solution(mesh):
    placed = (
        P(("group", "sample"), "member", None, "tile", None),
        P(("group", "sample"), None, None, "tile"),
        P(("group", "sample"), None, "tile"),
        P(("group", "sample"), "member"),
        P(),
        P(),
        P(),
        P(),
    )
    return jax.shard_map(
        on_device,
        mesh=mesh,
        in_specs=placed,
        out_specs=(
            P(("group", "sample"), None, "member", "tile"),
            P("group", None),
            P("group", None),
            P("group", None),
            P("group", None),
        ),
        check_vma=False,
    )
```

```python
import functools
import math

import jax
import jax.numpy as jnp
from jax import lax
from jax.experimental import pallas as pl
from jax.experimental.pallas import tpu as pltpu
from jax.sharding import PartitionSpec as P

gelu_coef = 0.7978845608028654
cubic_coef = 0.044715
soft_square = 0.0625
mesh_axes = ("member", "tile", "sample")
row_block = 8
point_chunk = 512
f32 = jnp.float32
bf16 = jnp.bfloat16


def rise_of(values):
    inner = jnp.tanh(values * (gelu_coef + gelu_coef * cubic_coef * (values * values)))
    return 0.5 + 0.5 * inner


def slope_of(values, rise):
    inside = values * (2.0 * gelu_coef + 6.0 * gelu_coef * cubic_coef * (values * values))
    return rise + rise * (1.0 - rise) * inside


def soft(values):
    return jnp.sqrt(values * values + soft_square)


def soft_slope(values):
    return values * lax.rsqrt(values * values + soft_square)


def forward_kernel(
    chunk, order, latent, observed, radar_valid, weight_in, weight_mid, weight_out, gains,
    latent_copy, observed_copy, valid_copy, pre_one, rise_one, hidden_one, pre_two, rise_two, hidden_two,
    predicted, sent, gain_row, mid_at, out_at, in_at, gains_at, sems, chunk_sems,
):
    block = latent_copy.shape[0]
    rows = observed_copy.shape[1]
    step = pl.program_id(0)
    here = pl.ds(pl.multiple_of(step * rows, rows), rows)
    pieces = []
    for number in range(block // chunk):
        source = latent.at[pl.ds(pl.multiple_of(step * block + number * chunk, chunk), chunk), :]
        into = latent_copy.at[pl.ds(number * chunk, chunk), :]
        pieces.append(pltpu.make_async_copy(source, into, chunk_sems.at[number]))
    pairs = [
        (weight_in, in_at), (gains, gains_at), (weight_mid, mid_at), (weight_out, out_at),
        (observed.at[:, here, :], observed_copy), (radar_valid.at[here, :], valid_copy),
    ]
    copies = [pltpu.make_async_copy(source, into, sems.at[k]) for k, (source, into) in enumerate(pairs)]
    copies[0].start()
    pieces[0].start()
    for copy in copies[1:4] + pieces[1:] + copies[4:]:
        copy.start()
    for number, piece in enumerate(pieces):
        spot = slice(number * chunk, (number + 1) * chunk)
        if number == 0:
            copies[0].wait()
        piece.wait()
        first = jnp.dot(latent_copy[spot, :], in_at[...], preferred_element_type=f32)
        rise = rise_of(first)
        if number == 0:
            for copy in copies[1:4]:
                copy.wait()
            gain = gains_at[pl.ds(order[0, 0], 1), :]
            gain_row[...] = gain
        pre_one[spot, :] = first
        rise_one[spot, :] = rise
        one = (first * rise * gain).astype(bf16)
        hidden_one[spot, :] = one
        second = jnp.dot(one, mid_at[...], preferred_element_type=f32)
        rise = rise_of(second)
        pre_two[spot, :] = second
        rise_two[spot, :] = rise
        two = (second * rise).astype(bf16)
        hidden_two[spot, :] = two
        last = lax.dot_general(out_at[...], two, (((1,), (1,)), ((), ())), preferred_element_type=f32)
        predicted[:, spot] = last
        sent[:, spot] = last.astype(bf16)
    for copy in copies[4:]:
        copy.wait()


def derivative_kernel(
    latent, observed, radar_valid, pre_one, rise_one, hidden_one, pre_two, rise_two, gain_row,
    act_one, slope_one, slope_two, latent_t, hidden_t, target, valid,
):
    cols = observed.shape[2]
    for row in range(observed.shape[1]):
        spot = slice(row * cols, (row + 1) * cols)
        target[:, spot] = observed[:, row, :]
        valid[:, spot] = radar_valid[row : row + 1, :].astype(f32)
    latent_t[...] = latent[...].T
    hidden_t[...] = hidden_one[...].T
    act_one[...] = pre_one[...] * rise_one[...]
    slope_one[...] = slope_of(pre_one[...], rise_one[...]) * gain_row[...]
    slope_two[...] = slope_of(pre_two[...], rise_two[...])


def backward_kernel(steps, scale_own, scale_pair, parts, order, *refs):
    (predicted, target, valid), refs = refs[:3], refs[3:]
    ensemble, refs = refs[:parts], refs[parts:]
    (latent_t, hidden_t, hidden_two, act_one, slope_one, slope_two, weight_mid, weight_out), refs = refs[:8], refs[8:]
    keep, away, rows = refs
    width, hidden = latent_t.shape[0], hidden_t.shape[0]
    fields = predicted.shape[0]
    half = keep.shape[0]
    step = pl.program_id(0)

    def put(first, count, value):
        if steps == 1:
            rows[first : first + count, :] = value
        else:
            rows[first : first + count, :] += value

    if steps > 1:

        @pl.when(step == 0)
        def _():
            rows[...] = jnp.zeros_like(rows)

    mine = predicted[...]
    slopes = None
    for part in ensemble:
        for k in range(part.shape[0]):
            one = soft_slope(mine - part[k].astype(f32))
            slopes = one if slopes is None else slopes + one
    grad = valid[...] * (soft_slope(mine - target[...]) * scale_own - slopes * scale_pair)
    flat = grad.astype(bf16)
    put(width + hidden, fields, jnp.dot(flat, hidden_two[...], preferred_element_type=f32))
    grad_hid_two = lax.dot_general(
        flat, weight_out[...], (((0,), (0,)), ((), ())), preferred_element_type=f32
    )
    grad_pre_two = (grad_hid_two * slope_two[...]).astype(bf16)
    grad_hid_one = lax.dot_general(
        grad_pre_two, weight_mid[...], (((1,), (1,)), ((), ())), preferred_element_type=f32
    )
    grad_pre_one = (grad_hid_one * slope_one[...]).astype(bf16)
    put(0, width, jnp.dot(latent_t[...], grad_pre_one, preferred_element_type=f32))
    put(width, hidden, jnp.dot(hidden_t[...], grad_pre_two, preferred_element_type=f32))
    gain_row = jnp.sum(grad_hid_one * act_one[...], axis=0, keepdims=True)
    first = width + hidden + fields
    count = rows.shape[0] - first
    spots = lax.broadcasted_iota(jnp.int32, (count, 1), 0)
    put(first, count, jnp.where(spots == order[0, 0], gain_row, 0.0))

    @pl.when(step == steps - 1)
    def _():
        which = half_of_device()
        keep[...] = rows[pl.ds(pl.multiple_of(which * half, 16), half), :]
        away[...] = rows[pl.ds(pl.multiple_of((1 - which) * half, 16), half), :]


def score_kernel(parts, predicted, target, valid, *refs):
    ensemble, score = refs[:parts], refs[parts]
    fields, rows, cols = score.shape
    here = pl.ds(pl.multiple_of(lax.axis_index("member") * (rows * cols), 128), rows * cols)
    blocks = [predicted[:, here]]
    for part in ensemble:
        for k in range(part.shape[0]):
            blocks.append(part[k, :, here].astype(f32))
    members = len(blocks)
    skill = sum(soft(block - target[:, here]) for block in blocks)
    if members <= 8:
        pairs = sum(soft(blocks[i] - blocks[j]) for i in range(members) for j in range(i))
    else:
        stack = jnp.stack(blocks)
        pairs = sum(jnp.sum(soft(stack[i + 1 :] - blocks[i]), axis=0) for i in range(members - 1))
    spread = 2.0 * pairs + members * math.sqrt(soft_square)
    value = valid[:, here] * (skill / members - spread / (2.0 * members * (members - 1)))
    for row in range(rows):
        score[:, row, :] = value[:, row * cols : (row + 1) * cols]


def output_kernel(total, other, grad_in, grad_mid, grad_out, grad_gains, sems):
    half = total.shape[0]
    moves = []
    first = 0
    for target in (grad_in, grad_mid, grad_out, grad_gains):
        last = first + target.shape[0]
        for side in range(2):
            low, high = max(first, side * half), min(last, (side + 1) * half)
            if low < high:
                moves.append((target, side, low - side * half, low - first, high - low))
        first = last

    def send(halves):
        copies = []
        for number, (target, side, source, into, count) in enumerate(moves):
            copy = pltpu.make_async_copy(
                halves[side].at[pl.ds(source, count), :], target.at[pl.ds(into, count), :], sems.at[number]
            )
            copy.start()
            copies.append(copy)
        for copy in copies:
            copy.wait()

    which = half_of_device()

    @pl.when(which == 0)
    def _():
        send((total, other))

    @pl.when(which != 0)
    def _():
        send((other, total))


def swap(array, offset):
    count = 1
    for axis in mesh_axes:
        count *= lax.axis_size(axis)
    return lax.ppermute(array, mesh_axes, [(place, place ^ offset) for place in range(count)])


def rounds_of(bits):
    return [bits[first : first + 2] for first in range(0, len(bits), 2)]


def bits_of(size, lowest):
    assert size & (size - 1) == 0
    return [lowest << place for place in range(size.bit_length() - 1)]


def gather_members(block):
    unit = lax.axis_size("tile") * lax.axis_size("sample")
    parts = [block[None]]
    for bits in rounds_of(bits_of(lax.axis_size("member"), unit)):
        whole = parts[0] if len(parts) == 1 else jnp.concatenate(parts)
        offsets = bits if len(bits) == 1 else [bits[0], bits[1], bits[0] ^ bits[1]]
        parts = parts + [swap(whole, offset) for offset in offsets]
    return parts[1:]


def reduction_bits():
    tiles, samples = lax.axis_size("tile"), lax.axis_size("sample")
    return bits_of(tiles, samples) + bits_of(lax.axis_size("member"), samples * tiles)


def half_of_device():
    place = lax.axis_index(mesh_axes)
    which = place & 1
    for bit in reduction_bits():
        which = which ^ jnp.where(place & bit, 1, 0)
    return which


def sum_parameters(keep, away, link_dtype):
    total = keep + swap(away, 1)
    for group in rounds_of(reduction_bits()):
        sent = total.astype(link_dtype)
        if len(group) == 1:
            arrived = swap(sent, group[0] ^ 1)
            total = sent.astype(f32) + arrived.astype(f32)
        else:
            near, far = group
            parts = [swap(sent, near ^ 1), swap(sent, far ^ 1), swap(sent, near ^ far)]
            parts = [part.astype(f32) for part in parts]
            total = (sent.astype(f32) + parts[0]) + (parts[1] + parts[2])
    return total, swap(total, 1)


def whole_spec(array):
    return pl.BlockSpec(array.shape, lambda step: (0,) * len(array.shape))


def block_spec(shape, block, axis):
    sizes = tuple(block if place == axis else size for place, size in enumerate(shape))
    return pl.BlockSpec(sizes, lambda step: tuple(step if place == axis else 0 for place in range(len(sizes))))


smem = pl.BlockSpec(memory_space=pltpu.SMEM)
kernel_params = pltpu.CompilerParams(vmem_limit_bytes=24 * 1024 * 1024)


def on_device(
    latent, observed, radar_valid, member_order, weight_in, weight_mid, weight_out, gains
):
    row_count = latent.shape[2]
    tile_cols = latent.shape[3]
    width = latent.shape[4]
    fields = weight_out.shape[1]
    hidden = weight_mid.shape[0]
    members = lax.axis_size("member")
    col_count = tile_cols * lax.axis_size("tile")
    points = row_count * tile_cols
    block_rows = min(row_count, row_block)
    block = block_rows * tile_cols
    steps = row_count // block_rows
    norm_factor = 1.0 / math.sqrt(lax.axis_size("sample") * row_count * col_count)
    inputs = latent[0, 0].reshape(points, width)
    weight_out_t = weight_out.T
    chunk = min(block, point_chunk)

    by_point = lambda shape: block_spec(shape, block, 0)
    by_lane = lambda shape: block_spec(shape, block, len(shape) - 1)
    result = pltpu.VMEM if steps == 1 else jax.ShapeDtypeStruct
    tall = lambda dtype: result((points, hidden), dtype)
    wide = lambda size, dtype: result((size, points), dtype)
    tall_spec = by_point((points, hidden))
    wide_spec = by_lane((fields, points))
    observed_spec = block_spec((fields, row_count, tile_cols), block_rows, 1)
    valid_spec = block_spec((row_count, tile_cols), block_rows, 0)
    gain_shape = result((1, hidden), f32)

    (latent_copy, observed_copy, valid_copy, pre_one, rise_one, hidden_one, pre_two, rise_two, hidden_two,
     predicted, sent, gain_row, mid_copy, out_copy) = pl.pallas_call(
        functools.partial(forward_kernel, chunk),
        grid=(steps,),
        in_specs=[smem] + [pl.BlockSpec(memory_space=pltpu.HBM)] * 7,
        out_specs=[by_point((points, width)), observed_spec, valid_spec]
        + [tall_spec] * 6 + [wide_spec] * 2
        + [whole_spec(array) for array in (gain_shape, weight_mid, weight_out_t)],
        out_shape=[
            result((points, width), bf16),
            result((fields, row_count, tile_cols), f32),
            result((row_count, tile_cols), jnp.int32),
            tall(f32), tall(f32), tall(bf16), tall(f32), tall(f32), tall(bf16),
            wide(fields, f32), wide(fields, bf16), gain_shape,
            result(weight_mid.shape, bf16), result(weight_out_t.shape, bf16),
        ],
        scratch_shapes=[pltpu.VMEM(array.shape, array.dtype) for array in (weight_in, gains)]
        + [pltpu.SemaphoreType.DMA((6,)), pltpu.SemaphoreType.DMA((block // chunk,))],
        compiler_params=kernel_params,
        name="forward",
    )(member_order, *[
        pltpu.with_memory_space_constraint(array, pltpu.HBM)
        for array in (inputs, observed[0], radar_valid[0], weight_in, weight_mid, weight_out_t, gains)
    ])

    parts = gather_members(sent)

    act_one, slope_one, slope_two, latent_t, hidden_t, target, is_valid = pl.pallas_call(
        derivative_kernel,
        grid=(steps,),
        in_specs=[by_point((points, width)), observed_spec, valid_spec]
        + [tall_spec] * 5 + [whole_spec(gain_shape)],
        out_specs=[tall_spec] * 3 + [by_lane((size, points)) for size in (width, hidden, fields, 1)],
        out_shape=[tall(f32)] * 3 + [wide(width, bf16), wide(hidden, bf16), wide(fields, f32), wide(1, f32)],
        compiler_params=kernel_params,
        name="derivatives",
    )(latent_copy, observed_copy, valid_copy, pre_one, rise_one, hidden_one, pre_two, rise_two, gain_row)

    used = width + hidden + fields + members
    half = -(-used // 32) * 16
    half_shape = jax.ShapeDtypeStruct((half, hidden), f32)
    keep, away = pl.pallas_call(
        functools.partial(
            backward_kernel,
            steps,
            norm_factor / members,
            norm_factor / (members * (members - 1.0)),
            len(parts),
        ),
        grid=(steps,),
        in_specs=[smem, wide_spec, wide_spec, by_lane((1, points))]
        + [by_lane(part.shape) for part in parts]
        + [by_lane((width, points)), by_lane((hidden, points))]
        + [tall_spec] * 4
        + [whole_spec(weight_mid), whole_spec(weight_out_t)],
        out_specs=[whole_spec(half_shape)] * 2,
        out_shape=[half_shape] * 2,
        scratch_shapes=[pltpu.VMEM((2 * half, hidden), f32)],
        compiler_params=kernel_params,
        name="backward",
    )(
        member_order, predicted, target, is_valid, *parts, latent_t, hidden_t,
        hidden_two, act_one, slope_one, slope_two, mid_copy, out_copy,
    )

    score_shape = jax.ShapeDtypeStruct((fields, row_count // members, tile_cols), f32)
    score_inputs = (predicted, target, is_valid, *parts)
    pixel_score = pl.pallas_call(
        functools.partial(score_kernel, len(parts)),
        grid=(1,),
        in_specs=[whole_spec(array) for array in score_inputs],
        out_specs=whole_spec(score_shape),
        out_shape=score_shape,
        compiler_params=kernel_params,
        name="score",
    )(*score_inputs)

    total, other = sum_parameters(keep, away, bf16)
    shapes = [jax.ShapeDtypeStruct((size, hidden), f32) for size in (width, hidden, fields, members)]
    grad_in, grad_mid, grad_out_t, grad_gains = pl.pallas_call(
        output_kernel,
        grid=(1,),
        in_specs=[whole_spec(total), whole_spec(other)],
        out_specs=[pl.BlockSpec(memory_space=pltpu.HBM)] * 4,
        out_shape=shapes,
        scratch_shapes=[pltpu.SemaphoreType.DMA((8,))],
        compiler_params=kernel_params,
        name="gradients",
    )(total, other)
    return (pixel_score[None], grad_in, grad_mid, grad_out_t.T, grad_gains)


def solution(mesh):
    placed = (
        P(("group", "sample"), "member", None, "tile", None),
        P(("group", "sample"), None, None, "tile"),
        P(("group", "sample"), None, "tile"),
        P(("group", "sample"), "member"),
        P(),
        P(),
        P(),
        P(),
    )
    return jax.shard_map(
        on_device,
        mesh=mesh,
        in_specs=placed,
        out_specs=(
            P(("group", "sample"), None, "member", "tile"),
            P("group", None),
            P("group", None),
            P("group", None),
            P("group", None),
        ),
        check_vma=False,
    )
```

```python
import functools
import math

import jax
import jax.numpy as jnp
from jax import lax
from jax.experimental import pallas as pl
from jax.experimental.pallas import tpu as pltpu
from jax.sharding import PartitionSpec as P

gelu_coef = 0.7978845608028654
cubic_coef = 0.044715
soft_square = 0.0625
mesh_axes = ("member", "tile", "sample")
row_block = 8
point_chunk = 1024
f32 = jnp.float32
bf16 = jnp.bfloat16


def rise_of(values):
    inner = jnp.tanh(values * (gelu_coef + gelu_coef * cubic_coef * (values * values)))
    return 0.5 + 0.5 * inner


def slope_of(values, rise):
    inside = values * (2.0 * gelu_coef + 6.0 * gelu_coef * cubic_coef * (values * values))
    return rise + rise * (1.0 - rise) * inside


def soft(values):
    return jnp.sqrt(values * values + soft_square)


def soft_slope(values):
    return values * lax.rsqrt(values * values + soft_square)


def forward_kernel(
    chunk, order, latent, observed, radar_valid, weight_in, weight_mid, weight_out, gains,
    latent_copy, observed_copy, valid_copy, pre_one, rise_one, hidden_one, pre_two, rise_two, hidden_two,
    predicted, sent, gain_row, mid_at, out_at, in_at, gains_at, sems, chunk_sems,
):
    block = latent_copy.shape[0]
    rows = observed_copy.shape[1]
    step = pl.program_id(0)
    here = pl.ds(pl.multiple_of(step * rows, rows), rows)
    pieces = []
    for number in range(block // chunk):
        source = latent.at[pl.ds(pl.multiple_of(step * block + number * chunk, chunk), chunk), :]
        into = latent_copy.at[pl.ds(number * chunk, chunk), :]
        pieces.append(pltpu.make_async_copy(source, into, chunk_sems.at[number]))
    pairs = [
        (weight_in, in_at), (gains, gains_at), (weight_mid, mid_at), (weight_out, out_at),
        (observed.at[:, here, :], observed_copy), (radar_valid.at[here, :], valid_copy),
    ]
    copies = [pltpu.make_async_copy(source, into, sems.at[k]) for k, (source, into) in enumerate(pairs)]
    copies[0].start()
    pieces[0].start()
    for copy in copies[1:4] + pieces[1:] + copies[4:]:
        copy.start()
    for number, piece in enumerate(pieces):
        spot = slice(number * chunk, (number + 1) * chunk)
        if number == 0:
            copies[0].wait()
        piece.wait()
        first = jnp.dot(latent_copy[spot, :], in_at[...], preferred_element_type=f32)
        rise = rise_of(first)
        if number == 0:
            for copy in copies[1:4]:
                copy.wait()
            gain = gains_at[pl.ds(order[0, 0], 1), :]
            gain_row[...] = gain
        pre_one[spot, :] = first
        rise_one[spot, :] = rise
        one = (first * rise * gain).astype(bf16)
        hidden_one[spot, :] = one
        second = jnp.dot(one, mid_at[...], preferred_element_type=f32)
        rise = rise_of(second)
        pre_two[spot, :] = second
        rise_two[spot, :] = rise
        two = (second * rise).astype(bf16)
        hidden_two[spot, :] = two
        last = lax.dot_general(out_at[...], two, (((1,), (1,)), ((), ())), preferred_element_type=f32)
        predicted[:, spot] = last
        sent[:, spot] = last.astype(bf16)
    for copy in copies[4:]:
        copy.wait()


def derivative_kernel(
    latent, observed, radar_valid, pre_one, rise_one, hidden_one, pre_two, rise_two, gain_row,
    act_one, slope_one, slope_two, latent_t, hidden_t, target, valid,
):
    cols = observed.shape[2]
    for row in range(observed.shape[1]):
        spot = slice(row * cols, (row + 1) * cols)
        target[:, spot] = observed[:, row, :]
        valid[:, spot] = radar_valid[row : row + 1, :].astype(f32)
    latent_t[...] = latent[...].T
    hidden_t[...] = hidden_one[...].T
    act_one[...] = pre_one[...] * rise_one[...]
    slope_one[...] = slope_of(pre_one[...], rise_one[...]) * gain_row[...]
    slope_two[...] = slope_of(pre_two[...], rise_two[...])


def backward_kernel(steps, scale_own, scale_pair, parts, order, *refs):
    (predicted, target, valid), refs = refs[:3], refs[3:]
    ensemble, refs = refs[:parts], refs[parts:]
    (latent_t, hidden_t, hidden_two, act_one, slope_one, slope_two, weight_mid, weight_out), refs = refs[:8], refs[8:]
    keep, away, rows = refs
    width, hidden = latent_t.shape[0], hidden_t.shape[0]
    fields = predicted.shape[0]
    half = keep.shape[0]
    step = pl.program_id(0)

    def put(first, count, value):
        if steps == 1:
            rows[first : first + count, :] = value
        else:
            rows[first : first + count, :] += value

    if steps > 1:

        @pl.when(step == 0)
        def _():
            rows[...] = jnp.zeros_like(rows)

    mine = predicted[...]
    slopes = None
    for part in ensemble:
        for k in range(part.shape[0]):
            one = soft_slope(mine - part[k].astype(f32))
            slopes = one if slopes is None else slopes + one
    grad = valid[...] * (soft_slope(mine - target[...]) * scale_own - slopes * scale_pair)
    flat = grad.astype(bf16)
    put(width + hidden, fields, jnp.dot(flat, hidden_two[...], preferred_element_type=f32))
    grad_hid_two = lax.dot_general(
        flat, weight_out[...], (((0,), (0,)), ((), ())), preferred_element_type=f32
    )
    grad_pre_two = (grad_hid_two * slope_two[...]).astype(bf16)
    grad_hid_one = lax.dot_general(
        grad_pre_two, weight_mid[...], (((1,), (1,)), ((), ())), preferred_element_type=f32
    )
    grad_pre_one = (grad_hid_one * slope_one[...]).astype(bf16)
    put(0, width, jnp.dot(latent_t[...], grad_pre_one, preferred_element_type=f32))
    put(width, hidden, jnp.dot(hidden_t[...], grad_pre_two, preferred_element_type=f32))
    gain_row = jnp.sum(grad_hid_one * act_one[...], axis=0, keepdims=True)
    first = width + hidden + fields
    count = rows.shape[0] - first
    spots = lax.broadcasted_iota(jnp.int32, (count, 1), 0)
    put(first, count, jnp.where(spots == order[0, 0], gain_row, 0.0))

    @pl.when(step == steps - 1)
    def _():
        which = half_of_device()
        keep[...] = rows[pl.ds(pl.multiple_of(which * half, 16), half), :]
        away[...] = rows[pl.ds(pl.multiple_of((1 - which) * half, 16), half), :]


def score_kernel(parts, predicted, target, valid, *refs):
    ensemble, score = refs[:parts], refs[parts]
    fields, rows, cols = score.shape
    here = pl.ds(pl.multiple_of(lax.axis_index("member") * (rows * cols), 128), rows * cols)
    blocks = [predicted[:, here]]
    for part in ensemble:
        for k in range(part.shape[0]):
            blocks.append(part[k, :, here].astype(f32))
    members = len(blocks)
    skill = sum(soft(block - target[:, here]) for block in blocks)
    if members <= 8:
        pairs = sum(soft(blocks[i] - blocks[j]) for i in range(members) for j in range(i))
    else:
        stack = jnp.stack(blocks)
        pairs = sum(jnp.sum(soft(stack[i + 1 :] - blocks[i]), axis=0) for i in range(members - 1))
    spread = 2.0 * pairs + members * math.sqrt(soft_square)
    value = valid[:, here] * (skill / members - spread / (2.0 * members * (members - 1)))
    for row in range(rows):
        score[:, row, :] = value[:, row * cols : (row + 1) * cols]


def output_kernel(total_in, other_in, grad_in, grad_mid, grad_out, grad_gains, total, other, sems):
    half = total.shape[0]
    total[...] = total_in[...].astype(f32)
    other[...] = other_in[...].astype(f32)
    moves = []
    first = 0
    for target in (grad_in, grad_mid, grad_out, grad_gains):
        last = first + target.shape[0]
        for side in range(2):
            low, high = max(first, side * half), min(last, (side + 1) * half)
            if low < high:
                moves.append((target, side, low - side * half, low - first, high - low))
        first = last

    def send(halves):
        copies = []
        for number, (target, side, source, into, count) in enumerate(moves):
            copy = pltpu.make_async_copy(
                halves[side].at[pl.ds(source, count), :], target.at[pl.ds(into, count), :], sems.at[number]
            )
            copy.start()
            copies.append(copy)
        for copy in copies:
            copy.wait()

    which = half_of_device()

    @pl.when(which == 0)
    def _():
        send((total, other))

    @pl.when(which != 0)
    def _():
        send((other, total))


def swap(array, offset):
    count = 1
    for axis in mesh_axes:
        count *= lax.axis_size(axis)
    return lax.ppermute(array, mesh_axes, [(place, place ^ offset) for place in range(count)])


def rounds_of(bits):
    return [bits[first : first + 2] for first in range(0, len(bits), 2)]


def bits_of(size, lowest):
    assert size & (size - 1) == 0
    return [lowest << place for place in range(size.bit_length() - 1)]


def gather_members(block):
    unit = lax.axis_size("tile") * lax.axis_size("sample")
    parts = [block[None]]
    for bits in rounds_of(bits_of(lax.axis_size("member"), unit)):
        whole = parts[0] if len(parts) == 1 else jnp.concatenate(parts)
        offsets = bits if len(bits) == 1 else [bits[0], bits[0] ^ bits[1], bits[1]]
        parts = parts + [swap(whole, offset) for offset in offsets]
    return parts[1:]


def reduction_bits():
    tiles, samples = lax.axis_size("tile"), lax.axis_size("sample")
    return bits_of(tiles, samples) + bits_of(lax.axis_size("member"), samples * tiles)


def flipped():
    return sum(reduction_bits())


def crossing(offset):
    return offset ^ (bin(offset & flipped()).count("1") & 1)


def half_of_device():
    place = lax.axis_index(mesh_axes)
    which = place & 1
    for bit in reduction_bits():
        if bit & flipped():
            which = which ^ jnp.where(place & bit, 1, 0)
    return which


def sum_parameters(keep, away, link_dtype):
    total = keep + swap(away.astype(bf16), 1).astype(f32)
    for group in rounds_of(reduction_bits()):
        sent = total.astype(link_dtype)
        if len(group) == 1:
            arrived = swap(sent, crossing(group[0]))
            total = sent.astype(f32) + arrived.astype(f32)
        else:
            near, far = group
            offsets = [near, far, near ^ far]
            got = {}
            for k in [0, 1, 2]:
                got[k] = swap(sent, crossing(offsets[k]))

            p = [got[k].astype(f32) for k in range(3)]
            total = (sent.astype(f32) + p[0]) + (p[1] + p[2])
    total = total.astype(bf16)
    return total, swap(total, 1)


def whole_spec(array):
    return pl.BlockSpec(array.shape, lambda step: (0,) * len(array.shape))


def block_spec(shape, block, axis):
    sizes = tuple(block if place == axis else size for place, size in enumerate(shape))
    return pl.BlockSpec(sizes, lambda step: tuple(step if place == axis else 0 for place in range(len(sizes))))


smem = pl.BlockSpec(memory_space=pltpu.SMEM)
kernel_params = pltpu.CompilerParams(vmem_limit_bytes=24 * 1024 * 1024)


def on_device(
    latent, observed, radar_valid, member_order, weight_in, weight_mid, weight_out, gains
):
    row_count = latent.shape[2]
    tile_cols = latent.shape[3]
    width = latent.shape[4]
    fields = weight_out.shape[1]
    hidden = weight_mid.shape[0]
    members = lax.axis_size("member")
    col_count = tile_cols * lax.axis_size("tile")
    points = row_count * tile_cols
    block_rows = min(row_count, row_block)
    block = block_rows * tile_cols
    steps = row_count // block_rows
    norm_factor = 1.0 / math.sqrt(lax.axis_size("sample") * row_count * col_count)
    inputs = latent[0, 0].reshape(points, width)
    weight_out_t = weight_out.T
    chunk = min(block, point_chunk)

    by_point = lambda shape: block_spec(shape, block, 0)
    by_lane = lambda shape: block_spec(shape, block, len(shape) - 1)
    result = pltpu.VMEM if steps == 1 else jax.ShapeDtypeStruct
    tall = lambda dtype: result((points, hidden), dtype)
    wide = lambda size, dtype: result((size, points), dtype)
    tall_spec = by_point((points, hidden))
    wide_spec = by_lane((fields, points))
    observed_spec = block_spec((fields, row_count, tile_cols), block_rows, 1)
    valid_spec = block_spec((row_count, tile_cols), block_rows, 0)
    gain_shape = result((1, hidden), f32)

    (latent_copy, observed_copy, valid_copy, pre_one, rise_one, hidden_one, pre_two, rise_two, hidden_two,
     predicted, sent, gain_row, mid_copy, out_copy) = pl.pallas_call(
        functools.partial(forward_kernel, chunk),
        grid=(steps,),
        in_specs=[smem] + [pl.BlockSpec(memory_space=pltpu.HBM)] * 7,
        out_specs=[by_point((points, width)), observed_spec, valid_spec]
        + [tall_spec] * 6 + [wide_spec] * 2
        + [whole_spec(array) for array in (gain_shape, weight_mid, weight_out_t)],
        out_shape=[
            result((points, width), bf16),
            result((fields, row_count, tile_cols), f32),
            result((row_count, tile_cols), jnp.int32),
            tall(f32), tall(f32), tall(bf16), tall(f32), tall(f32), tall(bf16),
            wide(fields, f32), wide(fields, bf16), gain_shape,
            result(weight_mid.shape, bf16), result(weight_out_t.shape, bf16),
        ],
        scratch_shapes=[pltpu.VMEM(array.shape, array.dtype) for array in (weight_in, gains)]
        + [pltpu.SemaphoreType.DMA((6,)), pltpu.SemaphoreType.DMA((block // chunk,))],
        compiler_params=kernel_params,
        name="forward",
    )(member_order, *[
        pltpu.with_memory_space_constraint(array, pltpu.HBM)
        for array in (inputs, observed[0], radar_valid[0], weight_in, weight_mid, weight_out_t, gains)
    ])

    parts = gather_members(sent)

    act_one, slope_one, slope_two, latent_t, hidden_t, target, is_valid = pl.pallas_call(
        derivative_kernel,
        grid=(steps,),
        in_specs=[by_point((points, width)), observed_spec, valid_spec]
        + [tall_spec] * 5 + [whole_spec(gain_shape)],
        out_specs=[tall_spec] * 3 + [by_lane((size, points)) for size in (width, hidden, fields, 1)],
        out_shape=[tall(f32)] * 3 + [wide(width, bf16), wide(hidden, bf16), wide(fields, f32), wide(1, f32)],
        compiler_params=kernel_params,
        name="derivatives",
    )(latent_copy, observed_copy, valid_copy, pre_one, rise_one, hidden_one, pre_two, rise_two, gain_row)

    used = width + hidden + fields + members
    half = -(-used // 32) * 16
    half_shape = jax.ShapeDtypeStruct((half, hidden), f32)
    keep, away = pl.pallas_call(
        functools.partial(
            backward_kernel,
            steps,
            norm_factor / members,
            norm_factor / (members * (members - 1.0)),
            len(parts),
        ),
        grid=(steps,),
        in_specs=[smem, wide_spec, wide_spec, by_lane((1, points))]
        + [by_lane(part.shape) for part in parts]
        + [by_lane((width, points)), by_lane((hidden, points))]
        + [tall_spec] * 4
        + [whole_spec(weight_mid), whole_spec(weight_out_t)],
        out_specs=[whole_spec(half_shape)] * 2,
        out_shape=[half_shape] * 2,
        scratch_shapes=[pltpu.VMEM((2 * half, hidden), f32)],
        compiler_params=kernel_params,
        name="backward",
    )(
        member_order, predicted, target, is_valid, *parts, latent_t, hidden_t,
        hidden_two, act_one, slope_one, slope_two, mid_copy, out_copy,
    )

    score_shape = jax.ShapeDtypeStruct((fields, row_count // members, tile_cols), f32)
    score_inputs = (predicted, target, is_valid, *parts)
    pixel_score = pl.pallas_call(
        functools.partial(score_kernel, len(parts)),
        grid=(1,),
        in_specs=[whole_spec(array) for array in score_inputs],
        out_specs=whole_spec(score_shape),
        out_shape=score_shape,
        compiler_params=kernel_params,
        name="score",
    )(*score_inputs)

    total, other = sum_parameters(keep, away, bf16)
    shapes = [jax.ShapeDtypeStruct((size, hidden), f32) for size in (width, hidden, fields, members)]
    grad_in, grad_mid, grad_out_t, grad_gains = pl.pallas_call(
        output_kernel,
        grid=(1,),
        in_specs=[whole_spec(total), whole_spec(other)],
        out_specs=[pl.BlockSpec(memory_space=pltpu.HBM)] * 4,
        out_shape=shapes,
        scratch_shapes=[pltpu.VMEM(total.shape, f32)] * 2 + [pltpu.SemaphoreType.DMA((8,))],
        compiler_params=kernel_params,
        name="gradients",
    )(total, other)
    return (pixel_score[None], grad_in, grad_mid, grad_out_t.T, grad_gains)


def solution(mesh):
    placed = (
        P(("group", "sample"), "member", None, "tile", None),
        P(("group", "sample"), None, None, "tile"),
        P(("group", "sample"), None, "tile"),
        P(("group", "sample"), "member"),
        P(),
        P(),
        P(),
        P(),
    )
    return jax.shard_map(
        on_device,
        mesh=mesh,
        in_specs=placed,
        out_specs=(
            P(("group", "sample"), None, "member", "tile"),
            P("group", None),
            P("group", None),
            P("group", None),
            P("group", None),
        ),
        check_vma=False,
    )
```

```python
import functools
import math

import jax
import jax.numpy as jnp
from jax import lax
from jax.experimental import pallas as pl
from jax.experimental.pallas import tpu as pltpu
from jax.sharding import PartitionSpec as P

gelu_coef = 0.7978845608028654
cubic_coef = 0.044715
soft_square = 0.0625
mesh_axes = ("member", "tile", "sample")
row_block = 8
point_chunk = 1024
f32 = jnp.float32
bf16 = jnp.bfloat16


def rise_of(values):
    inner = jnp.tanh(values * (gelu_coef + gelu_coef * cubic_coef * (values * values)))
    return 0.5 + 0.5 * inner


def slope_of(values, rise):
    inside = values * (2.0 * gelu_coef + 6.0 * gelu_coef * cubic_coef * (values * values))
    return rise + rise * (1.0 - rise) * inside


def soft(values):
    return jnp.sqrt(values * values + soft_square)


def soft_slope(values):
    return values * lax.rsqrt(values * values + soft_square)


def forward_kernel(
    chunk, order, latent, observed, radar_valid, weight_in, weight_mid, weight_out, gains,
    latent_copy, observed_copy, valid_copy, pre_one, rise_one, hidden_one, pre_two, rise_two, hidden_two,
    predicted, sent, gain_row, mid_at, out_at, in_at, gains_at, sems, chunk_sems,
):
    block = latent_copy.shape[0]
    rows = observed_copy.shape[1]
    step = pl.program_id(0)
    here = pl.ds(pl.multiple_of(step * rows, rows), rows)
    pieces = []
    for number in range(block // chunk):
        source = latent.at[pl.ds(pl.multiple_of(step * block + number * chunk, chunk), chunk), :]
        into = latent_copy.at[pl.ds(number * chunk, chunk), :]
        pieces.append(pltpu.make_async_copy(source, into, chunk_sems.at[number]))
    pairs = [
        (weight_in, in_at), (gains, gains_at), (weight_mid, mid_at), (weight_out, out_at),
        (observed.at[:, here, :], observed_copy), (radar_valid.at[here, :], valid_copy),
    ]
    copies = [pltpu.make_async_copy(source, into, sems.at[k]) for k, (source, into) in enumerate(pairs)]
    copies[0].start()
    pieces[0].start()
    for copy in copies[1:4] + pieces[1:] + copies[4:]:
        copy.start()
    for number, piece in enumerate(pieces):
        spot = slice(number * chunk, (number + 1) * chunk)
        if number == 0:
            copies[0].wait()
        piece.wait()
        first = jnp.dot(latent_copy[spot, :], in_at[...], preferred_element_type=f32)
        rise = rise_of(first)
        if number == 0:
            for copy in copies[1:4]:
                copy.wait()
            gain = gains_at[pl.ds(order[0, 0], 1), :]
            gain_row[...] = gain
        pre_one[spot, :] = first
        rise_one[spot, :] = rise
        one = (first * rise * gain).astype(bf16)
        hidden_one[spot, :] = one
        second = jnp.dot(one, mid_at[...], preferred_element_type=f32)
        rise = rise_of(second)
        pre_two[spot, :] = second
        rise_two[spot, :] = rise
        two = (second * rise).astype(bf16)
        hidden_two[spot, :] = two
        last = lax.dot_general(out_at[...], two, (((1,), (1,)), ((), ())), preferred_element_type=f32)
        predicted[:, spot] = last
        sent[:, spot] = last.astype(bf16)
    for copy in copies[4:]:
        copy.wait()


def derivative_kernel(
    latent, observed, radar_valid, pre_one, rise_one, hidden_one, pre_two, rise_two, gain_row,
    act_one, slope_one, slope_two, latent_t, hidden_t, target, valid,
):
    cols = observed.shape[2]
    for row in range(observed.shape[1]):
        spot = slice(row * cols, (row + 1) * cols)
        target[:, spot] = observed[:, row, :]
        valid[:, spot] = radar_valid[row : row + 1, :].astype(f32)
    latent_t[...] = latent[...].T
    hidden_t[...] = hidden_one[...].T
    act_one[...] = pre_one[...] * rise_one[...]
    slope_one[...] = slope_of(pre_one[...], rise_one[...]) * gain_row[...]
    slope_two[...] = slope_of(pre_two[...], rise_two[...])


def backward_kernel(steps, scale_own, scale_pair, parts, order, *refs):
    (predicted, target, valid), refs = refs[:3], refs[3:]
    ensemble, refs = refs[:parts], refs[parts:]
    (latent_t, hidden_t, hidden_two, act_one, slope_one, slope_two, weight_mid, weight_out), refs = refs[:8], refs[8:]
    keep, away, rows = refs
    width, hidden = latent_t.shape[0], hidden_t.shape[0]
    fields = predicted.shape[0]
    half = keep.shape[0]
    step = pl.program_id(0)

    def put(first, count, value):
        if steps == 1:
            rows[first : first + count, :] = value
        else:
            rows[first : first + count, :] += value

    if steps > 1:

        @pl.when(step == 0)
        def _():
            rows[...] = jnp.zeros_like(rows)

    mine = predicted[...]
    slopes = None
    for part in ensemble:
        for k in range(part.shape[0]):
            one = soft_slope(mine - part[k].astype(f32))
            slopes = one if slopes is None else slopes + one
    grad = valid[...] * (soft_slope(mine - target[...]) * scale_own - slopes * scale_pair)
    flat = grad.astype(bf16)
    put(width + hidden, fields, jnp.dot(flat, hidden_two[...], preferred_element_type=f32))
    grad_hid_two = lax.dot_general(
        flat, weight_out[...], (((0,), (0,)), ((), ())), preferred_element_type=f32
    )
    grad_pre_two = (grad_hid_two * slope_two[...]).astype(bf16)
    grad_hid_one = lax.dot_general(
        grad_pre_two, weight_mid[...], (((1,), (1,)), ((), ())), preferred_element_type=f32
    )
    grad_pre_one = (grad_hid_one * slope_one[...]).astype(bf16)
    put(0, width, jnp.dot(latent_t[...], grad_pre_one, preferred_element_type=f32))
    put(width, hidden, jnp.dot(hidden_t[...], grad_pre_two, preferred_element_type=f32))
    gain_row = jnp.sum(grad_hid_one * act_one[...], axis=0, keepdims=True)
    first = width + hidden + fields
    count = rows.shape[0] - first
    spots = lax.broadcasted_iota(jnp.int32, (count, 1), 0)
    put(first, count, jnp.where(spots == order[0, 0], gain_row, 0.0))

    @pl.when(step == steps - 1)
    def _():
        which = half_of_device()
        keep[...] = rows[pl.ds(pl.multiple_of(which * half, 16), half), :]
        away[...] = rows[pl.ds(pl.multiple_of((1 - which) * half, 16), half), :]


def score_kernel(parts, predicted, target, valid, *refs):
    ensemble, score = refs[:parts], refs[parts]
    fields, rows, cols = score.shape
    here = pl.ds(pl.multiple_of(lax.axis_index("member") * (rows * cols), 128), rows * cols)
    blocks = [predicted[:, here]]
    for part in ensemble:
        for k in range(part.shape[0]):
            blocks.append(part[k, :, here].astype(f32))
    members = len(blocks)
    skill = sum(soft(block - target[:, here]) for block in blocks)
    if members <= 8:
        pairs = sum(soft(blocks[i] - blocks[j]) for i in range(members) for j in range(i))
    else:
        stack = jnp.stack(blocks)
        pairs = sum(jnp.sum(soft(stack[i + 1 :] - blocks[i]), axis=0) for i in range(members - 1))
    spread = 2.0 * pairs + members * math.sqrt(soft_square)
    value = valid[:, here] * (skill / members - spread / (2.0 * members * (members - 1)))
    for row in range(rows):
        score[:, row, :] = value[:, row * cols : (row + 1) * cols]


def output_kernel(total, other, grad_in, grad_mid, grad_out, grad_gains, sems):
    half = total.shape[0]
    moves = []
    first = 0
    for target in (grad_in, grad_mid, grad_out, grad_gains):
        last = first + target.shape[0]
        for side in range(2):
            low, high = max(first, side * half), min(last, (side + 1) * half)
            if low < high:
                moves.append((target, side, low - side * half, low - first, high - low))
        first = last

    def send(halves):
        copies = []
        for number, (target, side, source, into, count) in enumerate(moves):
            copy = pltpu.make_async_copy(
                halves[side].at[pl.ds(source, count), :], target.at[pl.ds(into, count), :], sems.at[number]
            )
            copy.start()
            copies.append(copy)
        for copy in copies:
            copy.wait()

    which = half_of_device()

    @pl.when(which == 0)
    def _():
        send((total, other))

    @pl.when(which != 0)
    def _():
        send((other, total))


def swap(array, offset):
    count = 1
    for axis in mesh_axes:
        count *= lax.axis_size(axis)
    return lax.ppermute(array, mesh_axes, [(place, place ^ offset) for place in range(count)])


def rounds_of(bits):
    return [bits[first : first + 2] for first in range(0, len(bits), 2)]


def bits_of(size, lowest):
    assert size & (size - 1) == 0
    return [lowest << place for place in range(size.bit_length() - 1)]


def gather_members(block):
    members = lax.axis_size("member")
    if members == 4:
        routes = [(1, 0, 3, 2), (3, 2, 0, 1), (2, 3, 1, 0)]
        return [lax.ppermute(block[None], "member", list(enumerate(route))) for route in routes]
    unit = lax.axis_size("tile") * lax.axis_size("sample")
    parts = [block[None]]
    for bits in rounds_of(bits_of(members, unit)):
        whole = parts[0] if len(parts) == 1 else jnp.concatenate(parts)
        offsets = bits if len(bits) == 1 else [bits[0], bits[1], bits[0] ^ bits[1]]
        parts = parts + [swap(whole, offset) for offset in offsets]
    return parts[1:]


def chip_bits():
    tiles = lax.axis_size("tile")
    return bits_of(tiles, 1), bits_of(lax.axis_size("member"), tiles)


def turned(chip, chips):
    if chips == 8:
        return (41 >> chip) & 1
    value = 0
    for place in range(chips.bit_length() - 1):
        value = value ^ ((chip >> place) & 1)
    return value


def half_of_device():
    place = lax.axis_index(mesh_axes)
    return (place & 1) ^ turned(place >> 1, lax.axis_size("member") * lax.axis_size("tile"))


def cross(array, partner):
    chips = lax.axis_size("member") * lax.axis_size("tile")
    pairs = []
    for chip in range(chips):
        other = partner(chip)
        turn = turned(chip, chips) ^ turned(other, chips)
        pairs += [(2 * chip + core, 2 * other + (core ^ turn)) for core in range(2)]
    return lax.ppermute(array, mesh_axes, pairs)


def sum_parameters(keep, away, link_dtype):
    assert lax.axis_size("sample") == 2
    sent = (keep + swap(away, 1)).astype(link_dtype)
    tile_bits, member_bits = chip_bits()
    groups = rounds_of(tile_bits + member_bits)
    for place, group in enumerate(groups):
        if len(group) == 2:
            near, far = group
            one, two, three = (
                cross(sent, lambda chip: chip ^ offset).astype(f32) for offset in (near, far, near ^ far)
            )
            total = (sent.astype(f32) + one) + (two + three)
        else:
            turn = tile_bits[0] if place == len(groups) - 1 and place > 0 else 0
            odd = member_bits[0]
            arrived = cross(sent, lambda chip: chip ^ group[0] ^ (turn if chip & odd else 0))
            total = sent.astype(f32) + arrived.astype(f32)
        sent = total.astype(link_dtype)
    return total, swap(total, 1)


def whole_spec(array):
    return pl.BlockSpec(array.shape, lambda step: (0,) * len(array.shape))


def block_spec(shape, block, axis):
    sizes = tuple(block if place == axis else size for place, size in enumerate(shape))
    return pl.BlockSpec(sizes, lambda step: tuple(step if place == axis else 0 for place in range(len(sizes))))


smem = pl.BlockSpec(memory_space=pltpu.SMEM)
kernel_params = pltpu.CompilerParams(vmem_limit_bytes=24 * 1024 * 1024)


def on_device(
    latent, observed, radar_valid, member_order, weight_in, weight_mid, weight_out, gains
):
    row_count = latent.shape[2]
    tile_cols = latent.shape[3]
    width = latent.shape[4]
    fields = weight_out.shape[1]
    hidden = weight_mid.shape[0]
    members = lax.axis_size("member")
    col_count = tile_cols * lax.axis_size("tile")
    points = row_count * tile_cols
    block_rows = min(row_count, row_block)
    block = block_rows * tile_cols
    steps = row_count // block_rows
    norm_factor = 1.0 / math.sqrt(lax.axis_size("sample") * row_count * col_count)
    inputs = latent[0, 0].reshape(points, width)
    weight_out_t = weight_out.T
    chunk = min(block, point_chunk)

    by_point = lambda shape: block_spec(shape, block, 0)
    by_lane = lambda shape: block_spec(shape, block, len(shape) - 1)
    result = pltpu.VMEM if steps == 1 else jax.ShapeDtypeStruct
    tall = lambda dtype: result((points, hidden), dtype)
    wide = lambda size, dtype: result((size, points), dtype)
    tall_spec = by_point((points, hidden))
    wide_spec = by_lane((fields, points))
    observed_spec = block_spec((fields, row_count, tile_cols), block_rows, 1)
    valid_spec = block_spec((row_count, tile_cols), block_rows, 0)
    gain_shape = result((1, hidden), f32)

    (latent_copy, observed_copy, valid_copy, pre_one, rise_one, hidden_one, pre_two, rise_two, hidden_two,
     predicted, sent, gain_row, mid_copy, out_copy) = pl.pallas_call(
        functools.partial(forward_kernel, chunk),
        grid=(steps,),
        in_specs=[smem] + [pl.BlockSpec(memory_space=pltpu.HBM)] * 7,
        out_specs=[by_point((points, width)), observed_spec, valid_spec]
        + [tall_spec] * 6 + [wide_spec] * 2
        + [whole_spec(array) for array in (gain_shape, weight_mid, weight_out_t)],
        out_shape=[
            result((points, width), bf16),
            result((fields, row_count, tile_cols), f32),
            result((row_count, tile_cols), jnp.int32),
            tall(f32), tall(f32), tall(bf16), tall(f32), tall(f32), tall(bf16),
            wide(fields, f32), wide(fields, bf16), gain_shape,
            result(weight_mid.shape, bf16), result(weight_out_t.shape, bf16),
        ],
        scratch_shapes=[pltpu.VMEM(array.shape, array.dtype) for array in (weight_in, gains)]
        + [pltpu.SemaphoreType.DMA((6,)), pltpu.SemaphoreType.DMA((block // chunk,))],
        compiler_params=kernel_params,
        name="forward",
    )(member_order, *[
        pltpu.with_memory_space_constraint(array, pltpu.HBM)
        for array in (inputs, observed[0], radar_valid[0], weight_in, weight_mid, weight_out_t, gains)
    ])

    parts = gather_members(sent)

    act_one, slope_one, slope_two, latent_t, hidden_t, target, is_valid = pl.pallas_call(
        derivative_kernel,
        grid=(steps,),
        in_specs=[by_point((points, width)), observed_spec, valid_spec]
        + [tall_spec] * 5 + [whole_spec(gain_shape)],
        out_specs=[tall_spec] * 3 + [by_lane((size, points)) for size in (width, hidden, fields, 1)],
        out_shape=[tall(f32)] * 3 + [wide(width, bf16), wide(hidden, bf16), wide(fields, f32), wide(1, f32)],
        compiler_params=kernel_params,
        name="derivatives",
    )(latent_copy, observed_copy, valid_copy, pre_one, rise_one, hidden_one, pre_two, rise_two, gain_row)

    used = width + hidden + fields + members
    half = -(-used // 32) * 16
    half_shape = jax.ShapeDtypeStruct((half, hidden), f32)
    keep, away = pl.pallas_call(
        functools.partial(
            backward_kernel,
            steps,
            norm_factor / members,
            norm_factor / (members * (members - 1.0)),
            len(parts),
        ),
        grid=(steps,),
        in_specs=[smem, wide_spec, wide_spec, by_lane((1, points))]
        + [by_lane(part.shape) for part in parts]
        + [by_lane((width, points)), by_lane((hidden, points))]
        + [tall_spec] * 4
        + [whole_spec(weight_mid), whole_spec(weight_out_t)],
        out_specs=[whole_spec(half_shape)] * 2,
        out_shape=[half_shape] * 2,
        scratch_shapes=[pltpu.VMEM((2 * half, hidden), f32)],
        compiler_params=kernel_params,
        name="backward",
    )(
        member_order, predicted, target, is_valid, *parts, latent_t, hidden_t,
        hidden_two, act_one, slope_one, slope_two, mid_copy, out_copy,
    )

    score_shape = jax.ShapeDtypeStruct((fields, row_count // members, tile_cols), f32)
    score_inputs = (predicted, target, is_valid, *parts)
    pixel_score = pl.pallas_call(
        functools.partial(score_kernel, len(parts)),
        grid=(1,),
        in_specs=[whole_spec(array) for array in score_inputs],
        out_specs=whole_spec(score_shape),
        out_shape=score_shape,
        compiler_params=kernel_params,
        name="score",
    )(*score_inputs)

    total, other = sum_parameters(keep, away, bf16)
    shapes = [jax.ShapeDtypeStruct((size, hidden), f32) for size in (width, hidden, fields, members)]
    grad_in, grad_mid, grad_out_t, grad_gains = pl.pallas_call(
        output_kernel,
        grid=(1,),
        in_specs=[whole_spec(total), whole_spec(other)],
        out_specs=[pl.BlockSpec(memory_space=pltpu.HBM)] * 4,
        out_shape=shapes,
        scratch_shapes=[pltpu.SemaphoreType.DMA((8,))],
        compiler_params=kernel_params,
        name="gradients",
    )(total, other)
    return (pixel_score[None], grad_in, grad_mid, grad_out_t.T, grad_gains)


def solution(mesh):
    placed = (
        P(("group", "sample"), "member", None, "tile", None),
        P(("group", "sample"), None, None, "tile"),
        P(("group", "sample"), None, "tile"),
        P(("group", "sample"), "member"),
        P(),
        P(),
        P(),
        P(),
    )
    return jax.shard_map(
        on_device,
        mesh=mesh,
        in_specs=placed,
        out_specs=(
            P(("group", "sample"), None, "member", "tile"),
            P("group", None),
            P("group", None),
            P("group", None),
            P("group", None),
        ),
        check_vma=False,
    )
```

```python
import functools
import math

import jax
import jax.numpy as jnp
from jax import lax
from jax.experimental import pallas as pl
from jax.experimental.pallas import tpu as pltpu
from jax.sharding import PartitionSpec as P

gelu_coef = 0.7978845608028654
cubic_coef = 0.044715
soft_square = 0.0625
mesh_axes = ("member", "tile", "sample")
row_block = 8
point_chunk = 1024
f32 = jnp.float32
bf16 = jnp.bfloat16


def rise_of(values):
    inner = jnp.tanh(values * (gelu_coef + gelu_coef * cubic_coef * (values * values)))
    return 0.5 + 0.5 * inner


def slope_of(values, rise):
    inside = values * (2.0 * gelu_coef + 6.0 * gelu_coef * cubic_coef * (values * values))
    return rise + rise * (1.0 - rise) * inside


def soft(values):
    return jnp.sqrt(values * values + soft_square)


def soft_slope(values):
    return values * lax.rsqrt(values * values + soft_square)


def forward_kernel(
    chunk, order, latent, observed, radar_valid, weight_in, weight_mid, weight_out, gains,
    latent_copy, observed_copy, valid_copy, pre_one, rise_one, hidden_one, pre_two, rise_two, hidden_two,
    predicted, sent, gain_row, mid_at, out_at, in_at, gains_at, sems, chunk_sems,
):
    block = latent_copy.shape[0]
    rows = observed_copy.shape[1]
    step = pl.program_id(0)
    here = pl.ds(pl.multiple_of(step * rows, rows), rows)
    pieces = []
    for number in range(block // chunk):
        source = latent.at[pl.ds(pl.multiple_of(step * block + number * chunk, chunk), chunk), :]
        into = latent_copy.at[pl.ds(number * chunk, chunk), :]
        pieces.append(pltpu.make_async_copy(source, into, chunk_sems.at[number]))
    pairs = [
        (weight_in, in_at), (gains, gains_at), (weight_mid, mid_at), (weight_out, out_at),
        (observed.at[:, here, :], observed_copy), (radar_valid.at[here, :], valid_copy),
    ]
    copies = [pltpu.make_async_copy(source, into, sems.at[k]) for k, (source, into) in enumerate(pairs)]
    copies[0].start()
    pieces[0].start()
    for copy in copies[1:4] + pieces[1:] + copies[4:]:
        copy.start()
    for number, piece in enumerate(pieces):
        spot = slice(number * chunk, (number + 1) * chunk)
        if number == 0:
            copies[0].wait()
        piece.wait()
        first = jnp.dot(latent_copy[spot, :], in_at[...], preferred_element_type=f32)
        rise = rise_of(first)
        if number == 0:
            for copy in copies[1:4]:
                copy.wait()
            gain = gains_at[pl.ds(order[0, 0], 1), :]
            gain_row[...] = gain
        pre_one[spot, :] = first
        rise_one[spot, :] = rise
        one = (first * rise * gain).astype(bf16)
        hidden_one[spot, :] = one
        second = jnp.dot(one, mid_at[...], preferred_element_type=f32)
        rise = rise_of(second)
        pre_two[spot, :] = second
        rise_two[spot, :] = rise
        two = (second * rise).astype(bf16)
        hidden_two[spot, :] = two
        last = lax.dot_general(out_at[...], two, (((1,), (1,)), ((), ())), preferred_element_type=f32)
        predicted[:, spot] = last
        sent[:, spot] = last.astype(bf16)
    for copy in copies[4:]:
        copy.wait()


def derivative_kernel(
    latent, observed, radar_valid, pre_one, rise_one, hidden_one, pre_two, rise_two, gain_row,
    act_one, slope_one, slope_two, latent_t, hidden_t, target, valid,
):
    cols = observed.shape[2]
    for row in range(observed.shape[1]):
        spot = slice(row * cols, (row + 1) * cols)
        target[:, spot] = observed[:, row, :]
        valid[:, spot] = radar_valid[row : row + 1, :].astype(f32)
    latent_t[...] = latent[...].T
    hidden_t[...] = hidden_one[...].T
    act_one[...] = pre_one[...] * rise_one[...]
    slope_one[...] = slope_of(pre_one[...], rise_one[...]) * gain_row[...]
    slope_two[...] = slope_of(pre_two[...], rise_two[...])


def backward_kernel(steps, scale_own, scale_pair, parts, order, *refs):
    (predicted, target, valid), refs = refs[:3], refs[3:]
    ensemble, refs = refs[:parts], refs[parts:]
    (latent_t, hidden_t, hidden_two, act_one, slope_one, slope_two, weight_mid, weight_out), refs = refs[:8], refs[8:]
    keep, away, rows = refs
    width, hidden = latent_t.shape[0], hidden_t.shape[0]
    fields = predicted.shape[0]
    half = keep.shape[0]
    step = pl.program_id(0)

    def put(first, count, value):
        if steps == 1:
            rows[first : first + count, :] = value
        else:
            rows[first : first + count, :] += value

    if steps > 1:

        @pl.when(step == 0)
        def _():
            rows[...] = jnp.zeros_like(rows)

    mine = predicted[...]
    slopes = None
    for part in ensemble:
        for k in range(part.shape[0]):
            one = soft_slope(mine - part[k].astype(f32))
            slopes = one if slopes is None else slopes + one
    grad = valid[...] * (soft_slope(mine - target[...]) * scale_own - slopes * scale_pair)
    flat = grad.astype(bf16)
    put(width + hidden, fields, jnp.dot(flat, hidden_two[...], preferred_element_type=f32))
    grad_hid_two = lax.dot_general(
        flat, weight_out[...], (((0,), (0,)), ((), ())), preferred_element_type=f32
    )
    grad_pre_two = (grad_hid_two * slope_two[...]).astype(bf16)
    grad_hid_one = lax.dot_general(
        grad_pre_two, weight_mid[...], (((1,), (1,)), ((), ())), preferred_element_type=f32
    )
    grad_pre_one = (grad_hid_one * slope_one[...]).astype(bf16)
    put(0, width, jnp.dot(latent_t[...], grad_pre_one, preferred_element_type=f32))
    put(width, hidden, jnp.dot(hidden_t[...], grad_pre_two, preferred_element_type=f32))
    gain_row = jnp.sum(grad_hid_one * act_one[...], axis=0, keepdims=True)
    first = width + hidden + fields
    count = rows.shape[0] - first
    spots = lax.broadcasted_iota(jnp.int32, (count, 1), 0)
    put(first, count, jnp.where(spots == order[0, 0], gain_row, 0.0))

    @pl.when(step == steps - 1)
    def _():
        which = half_of_device()
        keep[...] = rows[pl.ds(pl.multiple_of(which * half, 8), half), :]
        away[...] = rows[pl.ds(pl.multiple_of((1 - which) * half, 8), half), :]


def score_kernel(parts, predicted, target, valid, *refs):
    ensemble, score = refs[:parts], refs[parts]
    fields, rows, cols = score.shape
    here = pl.ds(pl.multiple_of(lax.axis_index("member") * (rows * cols), 128), rows * cols)
    blocks = [predicted[:, here]]
    for part in ensemble:
        for k in range(part.shape[0]):
            blocks.append(part[k, :, here].astype(f32))
    members = len(blocks)
    skill = sum(soft(block - target[:, here]) for block in blocks)
    if members <= 8:
        pairs = sum(soft(blocks[i] - blocks[j]) for i in range(members) for j in range(i))
    else:
        stack = jnp.stack(blocks)
        pairs = sum(jnp.sum(soft(stack[i + 1 :] - blocks[i]), axis=0) for i in range(members - 1))
    spread = 2.0 * pairs + members * math.sqrt(soft_square)
    value = valid[:, here] * (skill / members - spread / (2.0 * members * (members - 1)))
    for row in range(rows):
        score[:, row, :] = value[:, row * cols : (row + 1) * cols]


def output_kernel(total, other, grad_in, grad_mid, grad_out, grad_gains, sems):
    half = total.shape[0]
    moves = []
    first = 0
    for target in (grad_in, grad_mid, grad_out, grad_gains):
        last = first + target.shape[0]
        for side in range(2):
            low, high = max(first, side * half), min(last, (side + 1) * half)
            if low < high:
                moves.append((target, side, low - side * half, low - first, high - low))
        first = last

    def send(halves):
        copies = []
        for number, (target, side, source, into, count) in enumerate(moves):
            copy = pltpu.make_async_copy(
                halves[side].at[pl.ds(source, count), :], target.at[pl.ds(into, count), :], sems.at[number]
            )
            copy.start()
            copies.append(copy)
        for copy in copies:
            copy.wait()

    which = half_of_device()

    @pl.when(which == 0)
    def _():
        send((total, other))

    @pl.when(which != 0)
    def _():
        send((other, total))


def swap(array, offset):
    count = 1
    for axis in mesh_axes:
        count *= lax.axis_size(axis)
    return lax.ppermute(array, mesh_axes, [(place, place ^ offset) for place in range(count)])


def rounds_of(bits):
    return [bits[first : first + 2] for first in range(0, len(bits), 2)]


def bits_of(size, lowest):
    assert size & (size - 1) == 0
    return [lowest << place for place in range(size.bit_length() - 1)]


def gather_members(block):
    members = lax.axis_size("member")
    if members == 4:
        routes = [(1, 0, 3, 2), (3, 2, 0, 1), (2, 3, 1, 0)]
        return [lax.ppermute(block[None], "member", list(enumerate(route))) for route in routes]
    unit = lax.axis_size("tile") * lax.axis_size("sample")
    parts = [block[None]]
    for bits in rounds_of(bits_of(members, unit)):
        whole = parts[0] if len(parts) == 1 else jnp.concatenate(parts)
        offsets = bits if len(bits) == 1 else [bits[0], bits[1], bits[0] ^ bits[1]]
        parts = parts + [swap(whole, offset) for offset in offsets]
    return parts[1:]


def chip_bits():
    tiles = lax.axis_size("tile")
    return bits_of(tiles, 1), bits_of(lax.axis_size("member"), tiles)


def turned(chip, chips):
    if chips == 8:
        return (41 >> chip) & 1
    value = 0
    for place in range(chips.bit_length() - 1):
        value = value ^ ((chip >> place) & 1)
    return value


def half_of_device():
    place = lax.axis_index(mesh_axes)
    return (place & 1) ^ turned(place >> 1, lax.axis_size("member") * lax.axis_size("tile"))


def cross(array, partner):
    chips = lax.axis_size("member") * lax.axis_size("tile")
    pairs = []
    for chip in range(chips):
        other = partner(chip)
        turn = turned(chip, chips) ^ turned(other, chips)
        pairs += [(2 * chip + core, 2 * other + (core ^ turn)) for core in range(2)]
    return lax.ppermute(array, mesh_axes, pairs)


def sum_parameters(keep, away, link_dtype):
    assert lax.axis_size("sample") == 2
    sent = (keep + swap(away, 1)).astype(link_dtype)
    tile_bits, member_bits = chip_bits()
    groups = rounds_of(tile_bits + member_bits)
    for place, group in enumerate(groups):
        if len(group) == 2:
            near, far = group
            one, two, three = (
                cross(sent, lambda chip: chip ^ offset).astype(f32) for offset in (near, far, near ^ far)
            )
            total = (sent.astype(f32) + one) + (two + three)
        else:
            turn = tile_bits[0] if place == len(groups) - 1 and place > 0 else 0
            odd = member_bits[0]
            arrived = cross(sent, lambda chip: chip ^ group[0] ^ (turn if chip & odd else 0))
            total = sent.astype(f32) + arrived.astype(f32)
        sent = total.astype(link_dtype)
    return total, swap(total, 1)


def whole_spec(array):
    return pl.BlockSpec(array.shape, lambda step: (0,) * len(array.shape))


def block_spec(shape, block, axis):
    sizes = tuple(block if place == axis else size for place, size in enumerate(shape))
    return pl.BlockSpec(sizes, lambda step: tuple(step if place == axis else 0 for place in range(len(sizes))))


smem = pl.BlockSpec(memory_space=pltpu.SMEM)
kernel_params = pltpu.CompilerParams(vmem_limit_bytes=24 * 1024 * 1024)


def on_device(
    latent, observed, radar_valid, member_order, weight_in, weight_mid, weight_out, gains
):
    row_count = latent.shape[2]
    tile_cols = latent.shape[3]
    width = latent.shape[4]
    fields = weight_out.shape[1]
    hidden = weight_mid.shape[0]
    members = lax.axis_size("member")
    col_count = tile_cols * lax.axis_size("tile")
    points = row_count * tile_cols
    block_rows = min(row_count, row_block)
    block = block_rows * tile_cols
    steps = row_count // block_rows
    norm_factor = 1.0 / math.sqrt(lax.axis_size("sample") * row_count * col_count)
    inputs = latent[0, 0].reshape(points, width)
    weight_out_t = weight_out.T
    chunk = min(block, point_chunk)

    by_point = lambda shape: block_spec(shape, block, 0)
    by_lane = lambda shape: block_spec(shape, block, len(shape) - 1)
    result = pltpu.VMEM if steps == 1 else jax.ShapeDtypeStruct
    tall = lambda dtype: result((points, hidden), dtype)
    wide = lambda size, dtype: result((size, points), dtype)
    tall_spec = by_point((points, hidden))
    wide_spec = by_lane((fields, points))
    observed_spec = block_spec((fields, row_count, tile_cols), block_rows, 1)
    valid_spec = block_spec((row_count, tile_cols), block_rows, 0)
    gain_shape = result((1, hidden), f32)

    (latent_copy, observed_copy, valid_copy, pre_one, rise_one, hidden_one, pre_two, rise_two, hidden_two,
     predicted, sent, gain_row, mid_copy, out_copy) = pl.pallas_call(
        functools.partial(forward_kernel, chunk),
        grid=(steps,),
        in_specs=[smem] + [pl.BlockSpec(memory_space=pltpu.HBM)] * 7,
        out_specs=[by_point((points, width)), observed_spec, valid_spec]
        + [tall_spec] * 6 + [wide_spec] * 2
        + [whole_spec(array) for array in (gain_shape, weight_mid, weight_out_t)],
        out_shape=[
            result((points, width), bf16),
            result((fields, row_count, tile_cols), f32),
            result((row_count, tile_cols), jnp.int32),
            tall(f32), tall(f32), tall(bf16), tall(f32), tall(f32), tall(bf16),
            wide(fields, f32), wide(fields, bf16), gain_shape,
            result(weight_mid.shape, bf16), result(weight_out_t.shape, bf16),
        ],
        scratch_shapes=[pltpu.VMEM(array.shape, array.dtype) for array in (weight_in, gains)]
        + [pltpu.SemaphoreType.DMA((6,)), pltpu.SemaphoreType.DMA((block // chunk,))],
        compiler_params=kernel_params,
        name="forward",
    )(member_order, *[
        pltpu.with_memory_space_constraint(array, pltpu.HBM)
        for array in (inputs, observed[0], radar_valid[0], weight_in, weight_mid, weight_out_t, gains)
    ])

    parts = gather_members(sent)

    act_one, slope_one, slope_two, latent_t, hidden_t, target, is_valid = pl.pallas_call(
        derivative_kernel,
        grid=(steps,),
        in_specs=[by_point((points, width)), observed_spec, valid_spec]
        + [tall_spec] * 5 + [whole_spec(gain_shape)],
        out_specs=[tall_spec] * 3 + [by_lane((size, points)) for size in (width, hidden, fields, 1)],
        out_shape=[tall(f32)] * 3 + [wide(width, bf16), wide(hidden, bf16), wide(fields, f32), wide(1, f32)],
        compiler_params=kernel_params,
        name="derivatives",
    )(latent_copy, observed_copy, valid_copy, pre_one, rise_one, hidden_one, pre_two, rise_two, gain_row)

    used = width + hidden + fields + members
    half = -(-used // 16) * 8
    half_shape = jax.ShapeDtypeStruct((half, hidden), f32)
    keep, away = pl.pallas_call(
        functools.partial(
            backward_kernel,
            steps,
            norm_factor / members,
            norm_factor / (members * (members - 1.0)),
            len(parts),
        ),
        grid=(steps,),
        in_specs=[smem, wide_spec, wide_spec, by_lane((1, points))]
        + [by_lane(part.shape) for part in parts]
        + [by_lane((width, points)), by_lane((hidden, points))]
        + [tall_spec] * 4
        + [whole_spec(weight_mid), whole_spec(weight_out_t)],
        out_specs=[whole_spec(half_shape)] * 2,
        out_shape=[half_shape] * 2,
        scratch_shapes=[pltpu.VMEM((2 * half, hidden), f32)],
        compiler_params=kernel_params,
        name="backward",
    )(
        member_order, predicted, target, is_valid, *parts, latent_t, hidden_t,
        hidden_two, act_one, slope_one, slope_two, mid_copy, out_copy,
    )

    score_shape = jax.ShapeDtypeStruct((fields, row_count // members, tile_cols), f32)
    score_inputs = (predicted, target, is_valid, *parts)
    pixel_score = pl.pallas_call(
        functools.partial(score_kernel, len(parts)),
        grid=(1,),
        in_specs=[whole_spec(array) for array in score_inputs],
        out_specs=whole_spec(score_shape),
        out_shape=score_shape,
        compiler_params=kernel_params,
        name="score",
    )(*score_inputs)

    total, other = sum_parameters(keep, away, bf16)
    shapes = [jax.ShapeDtypeStruct((size, hidden), f32) for size in (width, hidden, fields, members)]
    grad_in, grad_mid, grad_out_t, grad_gains = pl.pallas_call(
        output_kernel,
        grid=(1,),
        in_specs=[whole_spec(total), whole_spec(other)],
        out_specs=[pl.BlockSpec(memory_space=pltpu.HBM)] * 4,
        out_shape=shapes,
        scratch_shapes=[pltpu.SemaphoreType.DMA((8,))],
        compiler_params=kernel_params,
        name="gradients",
    )(total, other)
    return (pixel_score[None], grad_in, grad_mid, grad_out_t.T, grad_gains)


def solution(mesh):
    placed = (
        P(("group", "sample"), "member", None, "tile", None),
        P(("group", "sample"), None, None, "tile"),
        P(("group", "sample"), None, "tile"),
        P(("group", "sample"), "member"),
        P(),
        P(),
        P(),
        P(),
    )
    return jax.shard_map(
        on_device,
        mesh=mesh,
        in_specs=placed,
        out_specs=(
            P(("group", "sample"), None, "member", "tile"),
            P("group", None),
            P("group", None),
            P("group", None),
            P("group", None),
        ),
        check_vma=False,
    )
```

```python
import functools
import math

import jax
import jax.numpy as jnp
from jax import lax
from jax.experimental import pallas as pl
from jax.experimental.pallas import tpu as pltpu
from jax.sharding import PartitionSpec as P

gelu_coef = 0.7978845608028654
cubic_coef = 0.044715
soft_square = 0.0625
mesh_axes = ("member", "tile", "sample")
row_block = 8
point_chunk = 1024
f32 = jnp.float32
bf16 = jnp.bfloat16


def rise_of(values):
    inner = jnp.tanh(values * (gelu_coef + gelu_coef * cubic_coef * (values * values)))
    return 0.5 + 0.5 * inner


def slope_of(values, rise):
    inside = values * (2.0 * gelu_coef + 6.0 * gelu_coef * cubic_coef * (values * values))
    return rise + rise * (1.0 - rise) * inside


def soft(values):
    return jnp.sqrt(values * values + soft_square)


def soft_slope(values):
    return values * lax.rsqrt(values * values + soft_square)


def forward_kernel(
    chunk, order, latent, observed, radar_valid, weight_in, weight_mid, weight_out, gains,
    latent_copy, observed_copy, valid_copy, pre_one, rise_one, hidden_one, pre_two, rise_two, hidden_two,
    predicted, sent, gain_row, mid_at, out_at, in_at, gains_at, sems, chunk_sems,
):
    block = latent_copy.shape[0]
    rows = observed_copy.shape[1]
    step = pl.program_id(0)
    here = pl.ds(pl.multiple_of(step * rows, rows), rows)
    pieces = []
    for number in range(block // chunk):
        source = latent.at[pl.ds(pl.multiple_of(step * block + number * chunk, chunk), chunk), :]
        into = latent_copy.at[pl.ds(number * chunk, chunk), :]
        pieces.append(pltpu.make_async_copy(source, into, chunk_sems.at[number]))
    pairs = [
        (weight_in, in_at), (gains, gains_at), (weight_mid, mid_at), (weight_out, out_at),
        (observed.at[:, here, :], observed_copy), (radar_valid.at[here, :], valid_copy),
    ]
    copies = [pltpu.make_async_copy(source, into, sems.at[k]) for k, (source, into) in enumerate(pairs)]
    copies[0].start()
    pieces[0].start()
    for copy in copies[1:4] + pieces[1:] + copies[4:]:
        copy.start()
    for number, piece in enumerate(pieces):
        spot = slice(number * chunk, (number + 1) * chunk)
        if number == 0:
            copies[0].wait()
        piece.wait()
        first = jnp.dot(latent_copy[spot, :], in_at[...], preferred_element_type=f32)
        rise = rise_of(first)
        if number == 0:
            for copy in copies[1:4]:
                copy.wait()
            gain = gains_at[pl.ds(order[0, 0], 1), :]
            gain_row[...] = gain
        pre_one[spot, :] = first
        rise_one[spot, :] = rise
        one = (first * rise * gain).astype(bf16)
        hidden_one[spot, :] = one
        second = jnp.dot(one, mid_at[...], preferred_element_type=f32)
        rise = rise_of(second)
        pre_two[spot, :] = second
        rise_two[spot, :] = rise
        two = (second * rise).astype(bf16)
        hidden_two[spot, :] = two
        last = lax.dot_general(out_at[...], two, (((1,), (1,)), ((), ())), preferred_element_type=f32)
        predicted[:, spot] = last
        sent[:, spot] = last.astype(bf16)
    for copy in copies[4:]:
        copy.wait()


def derivative_kernel(
    latent, observed, radar_valid, pre_one, rise_one, hidden_one, pre_two, rise_two, gain_row,
    act_one, slope_one, slope_two, latent_t, hidden_t, target, valid,
):
    cols = observed.shape[2]
    for row in range(observed.shape[1]):
        spot = slice(row * cols, (row + 1) * cols)
        target[:, spot] = observed[:, row, :]
        valid[:, spot] = radar_valid[row : row + 1, :].astype(f32)
    latent_t[...] = latent[...].T
    hidden_t[...] = hidden_one[...].T
    act_one[...] = pre_one[...] * rise_one[...]
    slope_one[...] = slope_of(pre_one[...], rise_one[...]) * gain_row[...]
    slope_two[...] = slope_of(pre_two[...], rise_two[...])


def backward_kernel(steps, scale_own, scale_pair, parts, order, *refs):
    (predicted, target, valid), refs = refs[:3], refs[3:]
    ensemble, refs = refs[:parts], refs[parts:]
    (latent_t, hidden_t, hidden_two, act_one, slope_one, slope_two, weight_mid, weight_out), refs = refs[:8], refs[8:]
    keep, away, rows = refs
    width, hidden = latent_t.shape[0], hidden_t.shape[0]
    fields = predicted.shape[0]
    half = keep.shape[0]
    step = pl.program_id(0)

    def put(first, count, value):
        if steps == 1:
            rows[first : first + count, :] = value
        else:
            rows[first : first + count, :] += value

    if steps > 1:

        @pl.when(step == 0)
        def _():
            rows[...] = jnp.zeros_like(rows)

    mine = predicted[...]
    slopes = None
    for part in ensemble:
        for k in range(part.shape[0]):
            one = soft_slope(mine - part[k].astype(f32))
            slopes = one if slopes is None else slopes + one
    grad = valid[...] * (soft_slope(mine - target[...]) * scale_own - slopes * scale_pair)
    flat = grad.astype(bf16)
    put(width + hidden, fields, jnp.dot(flat, hidden_two[...], preferred_element_type=f32))
    grad_hid_two = lax.dot_general(
        flat, weight_out[...], (((0,), (0,)), ((), ())), preferred_element_type=f32
    )
    grad_pre_two = (grad_hid_two * slope_two[...]).astype(bf16)
    grad_hid_one = lax.dot_general(
        grad_pre_two, weight_mid[...], (((1,), (1,)), ((), ())), preferred_element_type=f32
    )
    grad_pre_one = (grad_hid_one * slope_one[...]).astype(bf16)
    put(0, width, jnp.dot(latent_t[...], grad_pre_one, preferred_element_type=f32))
    put(width, hidden, jnp.dot(hidden_t[...], grad_pre_two, preferred_element_type=f32))
    gain_row = jnp.sum(grad_hid_one * act_one[...], axis=0, keepdims=True)
    first = width + hidden + fields
    count = rows.shape[0] - first
    spots = lax.broadcasted_iota(jnp.int32, (count, 1), 0)
    put(first, count, jnp.where(spots == order[0, 0], gain_row, 0.0))

    @pl.when(step == steps - 1)
    def _():
        which = half_of_device()
        keep[...] = rows[pl.ds(pl.multiple_of(which * half, 8), half), :]
        away[...] = rows[pl.ds(pl.multiple_of((1 - which) * half, 8), half), :]


def fill_half(half_rows, side, order, latent_t, hidden_t, hidden_two, grad_pre_one, grad_pre_two, flat, gain_sum):
    half, width, hidden, fields = half_rows.shape[0], latent_t.shape[0], hidden_t.shape[0], flat.shape[0]
    if side == 0:
        upper = -(-half // 16) * 16
        part = jnp.dot(latent_t[0:upper, :], grad_pre_one[...], preferred_element_type=f32)
        half_rows[...] = part[:half]
        return
    lower = half // 16 * 16
    part = jnp.dot(latent_t[lower:width, :], grad_pre_one[...], preferred_element_type=f32)
    first = width - half
    half_rows[0:first, :] = part[half - lower :]
    half_rows[first : first + hidden, :] = jnp.dot(hidden_t[...], grad_pre_two[...], preferred_element_type=f32)
    first += hidden
    half_rows[first : first + fields, :] = jnp.dot(flat[...], hidden_two[...], preferred_element_type=f32)
    first += fields
    spots = lax.broadcasted_iota(jnp.int32, (half - first, 1), 0)
    half_rows[first:half, :] = jnp.where(spots == order[0, 0], gain_sum[...], 0.0)


def away_kernel(scale_own, scale_pair, parts, order, *refs):
    (predicted, target, valid), refs = refs[:3], refs[3:]
    ensemble, refs = refs[:parts], refs[parts:]
    latent_t, hidden_t, hidden_two, act_one, slope_one, slope_two, weight_mid, weight_out = refs[:8]
    away, grad_pre_one, grad_pre_two, flat, gain_sum = refs[8:]
    mine = predicted[...]
    slopes = sum(soft_slope(mine - part[0].astype(f32)) for part in ensemble)
    grad = valid[...] * (soft_slope(mine - target[...]) * scale_own - slopes * scale_pair)
    flat[...] = grad.astype(bf16)
    grad_hid_two = lax.dot_general(
        flat[...], weight_out[...], (((0,), (0,)), ((), ())), preferred_element_type=f32
    )
    grad_pre_two[...] = (grad_hid_two * slope_two[...]).astype(bf16)
    grad_hid_one = lax.dot_general(
        grad_pre_two[...], weight_mid[...], (((1,), (1,)), ((), ())), preferred_element_type=f32
    )
    grad_pre_one[...] = (grad_hid_one * slope_one[...]).astype(bf16)
    gain_sum[...] = jnp.sum(grad_hid_one * act_one[...], axis=0, keepdims=True)
    which = half_of_device()
    for side in range(2):

        @pl.when(which != side)
        def _():
            fill_half(away, side, order, latent_t, hidden_t, hidden_two, grad_pre_one, grad_pre_two, flat, gain_sum)


def keep_kernel(order, latent_t, hidden_t, hidden_two, grad_pre_one, grad_pre_two, flat, gain_sum, keep):
    which = half_of_device()
    for side in range(2):

        @pl.when(which == side)
        def _():
            fill_half(keep, side, order, latent_t, hidden_t, hidden_two, grad_pre_one, grad_pre_two, flat, gain_sum)


def score_kernel(parts, predicted, target, valid, *refs):
    ensemble, score = refs[:parts], refs[parts]
    fields, rows, cols = score.shape
    here = pl.ds(pl.multiple_of(lax.axis_index("member") * (rows * cols), 128), rows * cols)
    blocks = [predicted[:, here]]
    for part in ensemble:
        for k in range(part.shape[0]):
            blocks.append(part[k, :, here].astype(f32))
    members = len(blocks)
    skill = sum(soft(block - target[:, here]) for block in blocks)
    if members <= 8:
        pairs = sum(soft(blocks[i] - blocks[j]) for i in range(members) for j in range(i))
    else:
        stack = jnp.stack(blocks)
        pairs = sum(jnp.sum(soft(stack[i + 1 :] - blocks[i]), axis=0) for i in range(members - 1))
    spread = 2.0 * pairs + members * math.sqrt(soft_square)
    value = valid[:, here] * (skill / members - spread / (2.0 * members * (members - 1)))
    for row in range(rows):
        score[:, row, :] = value[:, row * cols : (row + 1) * cols]


def output_kernel(total, other, grad_in, grad_mid, grad_out, grad_gains, sems):
    half = total.shape[0]
    moves = []
    first = 0
    for target in (grad_in, grad_mid, grad_out, grad_gains):
        last = first + target.shape[0]
        for side in range(2):
            low, high = max(first, side * half), min(last, (side + 1) * half)
            if low < high:
                moves.append((target, side, low - side * half, low - first, high - low))
        first = last

    def send(halves):
        copies = []
        for number, (target, side, source, into, count) in enumerate(moves):
            copy = pltpu.make_async_copy(
                halves[side].at[pl.ds(source, count), :], target.at[pl.ds(into, count), :], sems.at[number]
            )
            copy.start()
            copies.append(copy)
        for copy in copies:
            copy.wait()

    which = half_of_device()

    @pl.when(which == 0)
    def _():
        send((total, other))

    @pl.when(which != 0)
    def _():
        send((other, total))


def swap(array, offset):
    count = 1
    for axis in mesh_axes:
        count *= lax.axis_size(axis)
    return lax.ppermute(array, mesh_axes, [(place, place ^ offset) for place in range(count)])


def rounds_of(bits):
    return [bits[first : first + 2] for first in range(0, len(bits), 2)]


def bits_of(size, lowest):
    assert size & (size - 1) == 0
    return [lowest << place for place in range(size.bit_length() - 1)]


def gather_members(block):
    members = lax.axis_size("member")
    if members == 4:
        routes = [(1, 0, 3, 2), (3, 2, 0, 1), (2, 3, 1, 0)]
        return [lax.ppermute(block[None], "member", list(enumerate(route))) for route in routes]
    unit = lax.axis_size("tile") * lax.axis_size("sample")
    parts = [block[None]]
    for bits in rounds_of(bits_of(members, unit)):
        whole = parts[0] if len(parts) == 1 else jnp.concatenate(parts)
        offsets = bits if len(bits) == 1 else [bits[0], bits[1], bits[0] ^ bits[1]]
        parts = parts + [swap(whole, offset) for offset in offsets]
    return parts[1:]


def chip_bits():
    tiles = lax.axis_size("tile")
    return bits_of(tiles, 1), bits_of(lax.axis_size("member"), tiles)


def turned(chip, chips):
    if chips == 8:
        return (41 >> chip) & 1
    value = 0
    for place in range(chips.bit_length() - 1):
        value = value ^ ((chip >> place) & 1)
    return value


def half_of_device():
    place = lax.axis_index(mesh_axes)
    return (place & 1) ^ turned(place >> 1, lax.axis_size("member") * lax.axis_size("tile"))


def cross(array, partner):
    chips = lax.axis_size("member") * lax.axis_size("tile")
    pairs = []
    for chip in range(chips):
        other = partner(chip)
        turn = turned(chip, chips) ^ turned(other, chips)
        pairs += [(2 * chip + core, 2 * other + (core ^ turn)) for core in range(2)]
    return lax.ppermute(array, mesh_axes, pairs)


def sum_parameters(keep, away, link_dtype):
    assert lax.axis_size("sample") == 2
    sent = (keep + swap(away, 1)).astype(link_dtype)
    tile_bits, member_bits = chip_bits()
    groups = rounds_of(tile_bits + member_bits)
    for place, group in enumerate(groups):
        if len(group) == 2:
            near, far = group
            one, two, three = (
                cross(sent, lambda chip: chip ^ offset).astype(f32) for offset in (near, far, near ^ far)
            )
            total = (sent.astype(f32) + one) + (two + three)
        else:
            turn = tile_bits[0] if place == len(groups) - 1 and place > 0 else 0
            odd = member_bits[0]
            arrived = cross(sent, lambda chip: chip ^ group[0] ^ (turn if chip & odd else 0))
            total = sent.astype(f32) + arrived.astype(f32)
        sent = total.astype(link_dtype)
    return total, swap(total, 1)


def whole_spec(array):
    return pl.BlockSpec(array.shape, lambda step: (0,) * len(array.shape))


def block_spec(shape, block, axis):
    sizes = tuple(block if place == axis else size for place, size in enumerate(shape))
    return pl.BlockSpec(sizes, lambda step: tuple(step if place == axis else 0 for place in range(len(sizes))))


smem = pl.BlockSpec(memory_space=pltpu.SMEM)
kernel_params = pltpu.CompilerParams(vmem_limit_bytes=24 * 1024 * 1024)


def on_device(
    latent, observed, radar_valid, member_order, weight_in, weight_mid, weight_out, gains
):
    row_count = latent.shape[2]
    tile_cols = latent.shape[3]
    width = latent.shape[4]
    fields = weight_out.shape[1]
    hidden = weight_mid.shape[0]
    members = lax.axis_size("member")
    col_count = tile_cols * lax.axis_size("tile")
    points = row_count * tile_cols
    block_rows = min(row_count, row_block)
    block = block_rows * tile_cols
    steps = row_count // block_rows
    norm_factor = 1.0 / math.sqrt(lax.axis_size("sample") * row_count * col_count)
    inputs = latent[0, 0].reshape(points, width)
    weight_out_t = weight_out.T
    chunk = min(block, point_chunk)

    by_point = lambda shape: block_spec(shape, block, 0)
    by_lane = lambda shape: block_spec(shape, block, len(shape) - 1)
    result = pltpu.VMEM if steps == 1 else jax.ShapeDtypeStruct
    tall = lambda dtype: result((points, hidden), dtype)
    wide = lambda size, dtype: result((size, points), dtype)
    tall_spec = by_point((points, hidden))
    wide_spec = by_lane((fields, points))
    observed_spec = block_spec((fields, row_count, tile_cols), block_rows, 1)
    valid_spec = block_spec((row_count, tile_cols), block_rows, 0)
    gain_shape = result((1, hidden), f32)

    (latent_copy, observed_copy, valid_copy, pre_one, rise_one, hidden_one, pre_two, rise_two, hidden_two,
     predicted, sent, gain_row, mid_copy, out_copy) = pl.pallas_call(
        functools.partial(forward_kernel, chunk),
        grid=(steps,),
        in_specs=[smem] + [pl.BlockSpec(memory_space=pltpu.HBM)] * 7,
        out_specs=[by_point((points, width)), observed_spec, valid_spec]
        + [tall_spec] * 6 + [wide_spec] * 2
        + [whole_spec(array) for array in (gain_shape, weight_mid, weight_out_t)],
        out_shape=[
            result((points, width), bf16),
            result((fields, row_count, tile_cols), f32),
            result((row_count, tile_cols), jnp.int32),
            tall(f32), tall(f32), tall(bf16), tall(f32), tall(f32), tall(bf16),
            wide(fields, f32), wide(fields, bf16), gain_shape,
            result(weight_mid.shape, bf16), result(weight_out_t.shape, bf16),
        ],
        scratch_shapes=[pltpu.VMEM(array.shape, array.dtype) for array in (weight_in, gains)]
        + [pltpu.SemaphoreType.DMA((6,)), pltpu.SemaphoreType.DMA((block // chunk,))],
        compiler_params=kernel_params,
        name="forward",
    )(member_order, *[
        pltpu.with_memory_space_constraint(array, pltpu.HBM)
        for array in (inputs, observed[0], radar_valid[0], weight_in, weight_mid, weight_out_t, gains)
    ])

    parts = gather_members(sent)

    act_one, slope_one, slope_two, latent_t, hidden_t, target, is_valid = pl.pallas_call(
        derivative_kernel,
        grid=(steps,),
        in_specs=[by_point((points, width)), observed_spec, valid_spec]
        + [tall_spec] * 5 + [whole_spec(gain_shape)],
        out_specs=[tall_spec] * 3 + [by_lane((size, points)) for size in (width, hidden, fields, 1)],
        out_shape=[tall(f32)] * 3 + [wide(width, bf16), wide(hidden, bf16), wide(fields, f32), wide(1, f32)],
        compiler_params=kernel_params,
        name="derivatives",
    )(latent_copy, observed_copy, valid_copy, pre_one, rise_one, hidden_one, pre_two, rise_two, gain_row)

    used = width + hidden + fields + members
    half = -(-used // 16) * 8
    half_shape = jax.ShapeDtypeStruct((half, hidden), f32)
    scales = (norm_factor / members, norm_factor / (members * (members - 1.0)), len(parts))
    if steps == 1 and all(part.shape[0] == 1 for part in parts) and half <= width:
        middle = [tall(bf16), tall(bf16), wide(fields, bf16), gain_shape]
        away, *middle_arrays = pl.pallas_call(
            functools.partial(away_kernel, *scales),
            grid=(steps,),
            in_specs=[smem, wide_spec, wide_spec, by_lane((1, points))]
            + [by_lane(part.shape) for part in parts]
            + [by_lane((width, points)), by_lane((hidden, points))]
            + [tall_spec] * 4
            + [whole_spec(weight_mid), whole_spec(weight_out_t)],
            out_specs=[whole_spec(half_shape)] + [whole_spec(shape) for shape in middle],
            out_shape=[half_shape] + middle,
            compiler_params=kernel_params,
            name="away",
        )(
            member_order, predicted, target, is_valid, *parts, latent_t, hidden_t,
            hidden_two, act_one, slope_one, slope_two, mid_copy, out_copy,
        )
        rest = (latent_t, hidden_t, hidden_two, *middle_arrays)
        keep = pl.pallas_call(
            keep_kernel,
            grid=(1,),
            in_specs=[smem] + [whole_spec(array) for array in rest],
            out_specs=whole_spec(half_shape),
            out_shape=half_shape,
            compiler_params=kernel_params,
            name="keep",
        )(member_order, *rest)
    else:
        keep, away = pl.pallas_call(
            functools.partial(
                backward_kernel,
                steps,
                norm_factor / members,
                norm_factor / (members * (members - 1.0)),
                len(parts),
            ),
            grid=(steps,),
            in_specs=[smem, wide_spec, wide_spec, by_lane((1, points))]
            + [by_lane(part.shape) for part in parts]
            + [by_lane((width, points)), by_lane((hidden, points))]
            + [tall_spec] * 4
            + [whole_spec(weight_mid), whole_spec(weight_out_t)],
            out_specs=[whole_spec(half_shape)] * 2,
            out_shape=[half_shape] * 2,
            scratch_shapes=[pltpu.VMEM((2 * half, hidden), f32)],
            compiler_params=kernel_params,
            name="backward",
        )(
            member_order, predicted, target, is_valid, *parts, latent_t, hidden_t,
            hidden_two, act_one, slope_one, slope_two, mid_copy, out_copy,
        )

    score_shape = jax.ShapeDtypeStruct((fields, row_count // members, tile_cols), f32)
    score_inputs = (predicted, target, is_valid, *parts)
    pixel_score = pl.pallas_call(
        functools.partial(score_kernel, len(parts)),
        grid=(1,),
        in_specs=[whole_spec(array) for array in score_inputs],
        out_specs=whole_spec(score_shape),
        out_shape=score_shape,
        compiler_params=kernel_params,
        name="score",
    )(*score_inputs)

    total, other = sum_parameters(keep, away, bf16)
    shapes = [jax.ShapeDtypeStruct((size, hidden), f32) for size in (width, hidden, fields, members)]
    grad_in, grad_mid, grad_out_t, grad_gains = pl.pallas_call(
        output_kernel,
        grid=(1,),
        in_specs=[whole_spec(total), whole_spec(other)],
        out_specs=[pl.BlockSpec(memory_space=pltpu.HBM)] * 4,
        out_shape=shapes,
        scratch_shapes=[pltpu.SemaphoreType.DMA((8,))],
        compiler_params=kernel_params,
        name="gradients",
    )(total, other)
    return (pixel_score[None], grad_in, grad_mid, grad_out_t.T, grad_gains)


def solution(mesh):
    placed = (
        P(("group", "sample"), "member", None, "tile", None),
        P(("group", "sample"), None, None, "tile"),
        P(("group", "sample"), None, "tile"),
        P(("group", "sample"), "member"),
        P(),
        P(),
        P(),
        P(),
    )
    return jax.shard_map(
        on_device,
        mesh=mesh,
        in_specs=placed,
        out_specs=(
            P(("group", "sample"), None, "member", "tile"),
            P("group", None),
            P("group", None),
            P("group", None),
            P("group", None),
        ),
        check_vma=False,
    )
```

```python
import functools
import math

import jax
import jax.numpy as jnp
from jax import lax
from jax.experimental import pallas as pl
from jax.experimental.pallas import tpu as pltpu
from jax.sharding import PartitionSpec as P

gelu_coef = 0.7978845608028654
cubic_coef = 0.044715
soft_square = 0.0625
mesh_axes = ("member", "tile", "sample")
row_block = 8
point_chunk = 1024
f32 = jnp.float32
bf16 = jnp.bfloat16


def rise_of(values):
    inner = jnp.tanh(values * (gelu_coef + gelu_coef * cubic_coef * (values * values)))
    return 0.5 + 0.5 * inner


def slope_of(values, rise):
    inside = values * (2.0 * gelu_coef + 6.0 * gelu_coef * cubic_coef * (values * values))
    return rise + rise * (1.0 - rise) * inside


def soft(values):
    return jnp.sqrt(values * values + soft_square)


def soft_slope(values):
    return values * lax.rsqrt(values * values + soft_square)


def forward_kernel(
    chunk, order, latent, observed, radar_valid, weight_in, weight_mid, weight_out, gains,
    latent_copy, observed_copy, valid_copy, pre_one, rise_one, hidden_one, pre_two, rise_two, hidden_two,
    predicted, sent, gain_row, mid_at, out_at, in_at, gains_at, sems, chunk_sems,
):
    block = latent_copy.shape[0]
    rows = observed_copy.shape[1]
    step = pl.program_id(0)
    here = pl.ds(pl.multiple_of(step * rows, rows), rows)
    pieces = []
    for number in range(block // chunk):
        source = latent.at[pl.ds(pl.multiple_of(step * block + number * chunk, chunk), chunk), :]
        into = latent_copy.at[pl.ds(number * chunk, chunk), :]
        pieces.append(pltpu.make_async_copy(source, into, chunk_sems.at[number]))
    pairs = [
        (weight_in, in_at), (gains, gains_at), (weight_mid, mid_at), (weight_out, out_at),
        (observed.at[:, here, :], observed_copy), (radar_valid.at[here, :], valid_copy),
    ]
    copies = [pltpu.make_async_copy(source, into, sems.at[k]) for k, (source, into) in enumerate(pairs)]
    copies[0].start()
    pieces[0].start()
    for copy in copies[1:4] + pieces[1:] + copies[4:]:
        copy.start()
    for number, piece in enumerate(pieces):
        spot = slice(number * chunk, (number + 1) * chunk)
        if number == 0:
            copies[0].wait()
        piece.wait()
        first = jnp.dot(latent_copy[spot, :], in_at[...], preferred_element_type=f32)
        rise = rise_of(first)
        if number == 0:
            for copy in copies[1:4]:
                copy.wait()
            gain = gains_at[pl.ds(order[0, 0], 1), :]
            gain_row[...] = gain
        pre_one[spot, :] = first
        rise_one[spot, :] = rise
        one = (first * rise * gain).astype(bf16)
        hidden_one[spot, :] = one
        second = jnp.dot(one, mid_at[...], preferred_element_type=f32)
        rise = rise_of(second)
        pre_two[spot, :] = second
        rise_two[spot, :] = rise
        two = (second * rise).astype(bf16)
        hidden_two[spot, :] = two
        last = lax.dot_general(out_at[...], two, (((1,), (1,)), ((), ())), preferred_element_type=f32)
        predicted[:, spot] = last
        sent[:, spot] = last.astype(bf16)
    for copy in copies[4:]:
        copy.wait()


def derivative_kernel(
    latent, observed, radar_valid, pre_one, rise_one, hidden_one, pre_two, rise_two, gain_row,
    act_one, slope_one, slope_two, latent_t, hidden_t, target, valid,
):
    cols = observed.shape[2]
    for row in range(observed.shape[1]):
        spot = slice(row * cols, (row + 1) * cols)
        target[:, spot] = observed[:, row, :]
        valid[:, spot] = radar_valid[row : row + 1, :].astype(f32)
    latent_t[...] = latent[...].T
    hidden_t[...] = hidden_one[...].T
    act_one[...] = pre_one[...] * rise_one[...]
    slope_one[...] = slope_of(pre_one[...], rise_one[...]) * gain_row[...]
    slope_two[...] = slope_of(pre_two[...], rise_two[...])


def backward_kernel(steps, scale_own, scale_pair, parts, order, *refs):
    (predicted, target, valid), refs = refs[:3], refs[3:]
    ensemble, refs = refs[:parts], refs[parts:]
    (latent_t, hidden_t, hidden_two, act_one, slope_one, slope_two, weight_mid, weight_out), refs = refs[:8], refs[8:]
    keep, away, rows = refs
    width, hidden = latent_t.shape[0], hidden_t.shape[0]
    fields = predicted.shape[0]
    half = keep.shape[0]
    step = pl.program_id(0)

    def put(first, count, value):
        if steps == 1:
            rows[first : first + count, :] = value
        else:
            rows[first : first + count, :] += value

    if steps > 1:

        @pl.when(step == 0)
        def _():
            rows[...] = jnp.zeros_like(rows)

    mine = predicted[...]
    slopes = None
    for part in ensemble:
        for k in range(part.shape[0]):
            one = soft_slope(mine - part[k].astype(f32))
            slopes = one if slopes is None else slopes + one
    grad = valid[...] * (soft_slope(mine - target[...]) * scale_own - slopes * scale_pair)
    flat = grad.astype(bf16)
    put(width + hidden, fields, jnp.dot(flat, hidden_two[...], preferred_element_type=f32))
    grad_hid_two = lax.dot_general(
        flat, weight_out[...], (((0,), (0,)), ((), ())), preferred_element_type=f32
    )
    grad_pre_two = (grad_hid_two * slope_two[...]).astype(bf16)
    grad_hid_one = lax.dot_general(
        grad_pre_two, weight_mid[...], (((1,), (1,)), ((), ())), preferred_element_type=f32
    )
    grad_pre_one = (grad_hid_one * slope_one[...]).astype(bf16)
    put(0, width, jnp.dot(latent_t[...], grad_pre_one, preferred_element_type=f32))
    put(width, hidden, jnp.dot(hidden_t[...], grad_pre_two, preferred_element_type=f32))
    gain_row = jnp.sum(grad_hid_one * act_one[...], axis=0, keepdims=True)
    first = width + hidden + fields
    count = rows.shape[0] - first
    spots = lax.broadcasted_iota(jnp.int32, (count, 1), 0)
    put(first, count, jnp.where(spots == order[0, 0], gain_row, 0.0))

    @pl.when(step == steps - 1)
    def _():
        which = half_of_device()
        keep[...] = rows[pl.ds(pl.multiple_of(which * half, 8), half), :]
        away[...] = rows[pl.ds(pl.multiple_of((1 - which) * half, 8), half), :]


def score_kernel(parts, predicted, target, valid, *refs):
    ensemble, score = refs[:parts], refs[parts]
    fields, rows, cols = score.shape
    here = pl.ds(pl.multiple_of(lax.axis_index("member") * (rows * cols), 128), rows * cols)
    blocks = [predicted[:, here]]
    for part in ensemble:
        for k in range(part.shape[0]):
            blocks.append(part[k, :, here].astype(f32))
    members = len(blocks)
    skill = sum(soft(block - target[:, here]) for block in blocks)
    if members <= 8:
        pairs = sum(soft(blocks[i] - blocks[j]) for i in range(members) for j in range(i))
    else:
        stack = jnp.stack(blocks)
        pairs = sum(jnp.sum(soft(stack[i + 1 :] - blocks[i]), axis=0) for i in range(members - 1))
    spread = 2.0 * pairs + members * math.sqrt(soft_square)
    value = valid[:, here] * (skill / members - spread / (2.0 * members * (members - 1)))
    for row in range(rows):
        score[:, row, :] = value[:, row * cols : (row + 1) * cols]


def output_kernel(total, other, grad_in, grad_mid, grad_out, grad_gains, sems):
    half = total.shape[0]
    moves = []
    first = 0
    for target in (grad_in, grad_mid, grad_out, grad_gains):
        last = first + target.shape[0]
        for side in range(2):
            low, high = max(first, side * half), min(last, (side + 1) * half)
            if low < high:
                moves.append((target, side, low - side * half, low - first, high - low))
        first = last

    def send(halves):
        copies = []
        for number, (target, side, source, into, count) in enumerate(moves):
            copy = pltpu.make_async_copy(
                halves[side].at[pl.ds(source, count), :], target.at[pl.ds(into, count), :], sems.at[number]
            )
            copy.start()
            copies.append(copy)
        for copy in copies:
            copy.wait()

    which = half_of_device()

    @pl.when(which == 0)
    def _():
        send((total, other))

    @pl.when(which != 0)
    def _():
        send((other, total))


def swap(array, offset):
    count = 1
    for axis in mesh_axes:
        count *= lax.axis_size(axis)
    return lax.ppermute(array, mesh_axes, [(place, place ^ offset) for place in range(count)])


def rounds_of(bits):
    return [bits[first : first + 2] for first in range(0, len(bits), 2)]


def bits_of(size, lowest):
    assert size & (size - 1) == 0
    return [lowest << place for place in range(size.bit_length() - 1)]


def gather_members(block):
    members = lax.axis_size("member")
    if members == 4:
        routes = [(1, 0, 3, 2), (3, 2, 0, 1), (2, 3, 1, 0)]
        return [lax.ppermute(block[None], "member", list(enumerate(route))) for route in routes]
    unit = lax.axis_size("tile") * lax.axis_size("sample")
    parts = [block[None]]
    for bits in rounds_of(bits_of(members, unit)):
        whole = parts[0] if len(parts) == 1 else jnp.concatenate(parts)
        offsets = bits if len(bits) == 1 else [bits[0], bits[1], bits[0] ^ bits[1]]
        parts = parts + [swap(whole, offset) for offset in offsets]
    return parts[1:]


def chip_bits():
    tiles = lax.axis_size("tile")
    return bits_of(tiles, 1), bits_of(lax.axis_size("member"), tiles)


def turned(chip, chips):
    if chips == 8:
        return (41 >> chip) & 1
    value = 0
    for place in range(chips.bit_length() - 1):
        value = value ^ ((chip >> place) & 1)
    return value


def half_of_device():
    place = lax.axis_index(mesh_axes)
    return (place & 1) ^ turned(place >> 1, lax.axis_size("member") * lax.axis_size("tile"))


def cross(array, partner):
    chips = lax.axis_size("member") * lax.axis_size("tile")
    pairs = []
    for chip in range(chips):
        other = partner(chip)
        turn = turned(chip, chips) ^ turned(other, chips)
        pairs += [(2 * chip + core, 2 * other + (core ^ turn)) for core in range(2)]
    return lax.ppermute(array, mesh_axes, pairs)


def sum_parameters(keep, away, link_dtype):
    assert lax.axis_size("sample") == 2
    sent = (keep + swap(away.astype(link_dtype), 1).astype(f32)).astype(link_dtype)
    tile_bits, member_bits = chip_bits()
    groups = rounds_of(tile_bits + member_bits)
    for place, group in enumerate(groups):
        if len(group) == 2:
            near, far = group
            one, two, three = (
                cross(sent, lambda chip: chip ^ offset).astype(f32) for offset in (near, far, near ^ far)
            )
            total = (sent.astype(f32) + one) + (two + three)
        else:
            turn = tile_bits[0] if place == len(groups) - 1 and place > 0 else 0
            odd = member_bits[0]
            arrived = cross(sent, lambda chip: chip ^ group[0] ^ (turn if chip & odd else 0))
            total = sent.astype(f32) + arrived.astype(f32)
        sent = total.astype(link_dtype)
    return total, swap(total, 1)


def whole_spec(array):
    return pl.BlockSpec(array.shape, lambda step: (0,) * len(array.shape))


def block_spec(shape, block, axis):
    sizes = tuple(block if place == axis else size for place, size in enumerate(shape))
    return pl.BlockSpec(sizes, lambda step: tuple(step if place == axis else 0 for place in range(len(sizes))))


smem = pl.BlockSpec(memory_space=pltpu.SMEM)
kernel_params = pltpu.CompilerParams(vmem_limit_bytes=24 * 1024 * 1024)


def on_device(
    latent, observed, radar_valid, member_order, weight_in, weight_mid, weight_out, gains
):
    row_count = latent.shape[2]
    tile_cols = latent.shape[3]
    width = latent.shape[4]
    fields = weight_out.shape[1]
    hidden = weight_mid.shape[0]
    members = lax.axis_size("member")
    col_count = tile_cols * lax.axis_size("tile")
    points = row_count * tile_cols
    block_rows = min(row_count, row_block)
    block = block_rows * tile_cols
    steps = row_count // block_rows
    norm_factor = 1.0 / math.sqrt(lax.axis_size("sample") * row_count * col_count)
    inputs = latent[0, 0].reshape(points, width)
    weight_out_t = weight_out.T
    chunk = min(block, point_chunk)

    by_point = lambda shape: block_spec(shape, block, 0)
    by_lane = lambda shape: block_spec(shape, block, len(shape) - 1)
    result = pltpu.VMEM if steps == 1 else jax.ShapeDtypeStruct
    tall = lambda dtype: result((points, hidden), dtype)
    wide = lambda size, dtype: result((size, points), dtype)
    tall_spec = by_point((points, hidden))
    wide_spec = by_lane((fields, points))
    observed_spec = block_spec((fields, row_count, tile_cols), block_rows, 1)
    valid_spec = block_spec((row_count, tile_cols), block_rows, 0)
    gain_shape = result((1, hidden), f32)

    (latent_copy, observed_copy, valid_copy, pre_one, rise_one, hidden_one, pre_two, rise_two, hidden_two,
     predicted, sent, gain_row, mid_copy, out_copy) = pl.pallas_call(
        functools.partial(forward_kernel, chunk),
        grid=(steps,),
        in_specs=[smem] + [pl.BlockSpec(memory_space=pltpu.HBM)] * 7,
        out_specs=[by_point((points, width)), observed_spec, valid_spec]
        + [tall_spec] * 6 + [wide_spec] * 2
        + [whole_spec(array) for array in (gain_shape, weight_mid, weight_out_t)],
        out_shape=[
            result((points, width), bf16),
            result((fields, row_count, tile_cols), f32),
            result((row_count, tile_cols), jnp.int32),
            tall(f32), tall(f32), tall(bf16), tall(f32), tall(f32), tall(bf16),
            wide(fields, f32), wide(fields, bf16), gain_shape,
            result(weight_mid.shape, bf16), result(weight_out_t.shape, bf16),
        ],
        scratch_shapes=[pltpu.VMEM(array.shape, array.dtype) for array in (weight_in, gains)]
        + [pltpu.SemaphoreType.DMA((6,)), pltpu.SemaphoreType.DMA((block // chunk,))],
        compiler_params=kernel_params,
        name="forward",
    )(member_order, *[
        pltpu.with_memory_space_constraint(array, pltpu.HBM)
        for array in (inputs, observed[0], radar_valid[0], weight_in, weight_mid, weight_out_t, gains)
    ])

    parts = gather_members(sent)

    act_one, slope_one, slope_two, latent_t, hidden_t, target, is_valid = pl.pallas_call(
        derivative_kernel,
        grid=(steps,),
        in_specs=[by_point((points, width)), observed_spec, valid_spec]
        + [tall_spec] * 5 + [whole_spec(gain_shape)],
        out_specs=[tall_spec] * 3 + [by_lane((size, points)) for size in (width, hidden, fields, 1)],
        out_shape=[tall(f32)] * 3 + [wide(width, bf16), wide(hidden, bf16), wide(fields, f32), wide(1, f32)],
        compiler_params=kernel_params,
        name="derivatives",
    )(latent_copy, observed_copy, valid_copy, pre_one, rise_one, hidden_one, pre_two, rise_two, gain_row)

    used = width + hidden + fields + members
    half = -(-used // 16) * 8
    half_shape = jax.ShapeDtypeStruct((half, hidden), f32)
    keep, away = pl.pallas_call(
        functools.partial(
            backward_kernel,
            steps,
            norm_factor / members,
            norm_factor / (members * (members - 1.0)),
            len(parts),
        ),
        grid=(steps,),
        in_specs=[smem, wide_spec, wide_spec, by_lane((1, points))]
        + [by_lane(part.shape) for part in parts]
        + [by_lane((width, points)), by_lane((hidden, points))]
        + [tall_spec] * 4
        + [whole_spec(weight_mid), whole_spec(weight_out_t)],
        out_specs=[whole_spec(half_shape)] * 2,
        out_shape=[half_shape] * 2,
        scratch_shapes=[pltpu.VMEM((2 * half, hidden), f32)],
        compiler_params=kernel_params,
        name="backward",
    )(
        member_order, predicted, target, is_valid, *parts, latent_t, hidden_t,
        hidden_two, act_one, slope_one, slope_two, mid_copy, out_copy,
    )

    score_shape = jax.ShapeDtypeStruct((fields, row_count // members, tile_cols), f32)
    score_inputs = (predicted, target, is_valid, *parts)
    pixel_score = pl.pallas_call(
        functools.partial(score_kernel, len(parts)),
        grid=(1,),
        in_specs=[whole_spec(array) for array in score_inputs],
        out_specs=whole_spec(score_shape),
        out_shape=score_shape,
        compiler_params=kernel_params,
        name="score",
    )(*score_inputs)

    total, other = sum_parameters(keep, away, bf16)
    shapes = [jax.ShapeDtypeStruct((size, hidden), f32) for size in (width, hidden, fields, members)]
    grad_in, grad_mid, grad_out_t, grad_gains = pl.pallas_call(
        output_kernel,
        grid=(1,),
        in_specs=[whole_spec(total), whole_spec(other)],
        out_specs=[pl.BlockSpec(memory_space=pltpu.HBM)] * 4,
        out_shape=shapes,
        scratch_shapes=[pltpu.SemaphoreType.DMA((8,))],
        compiler_params=kernel_params,
        name="gradients",
    )(total, other)
    return (pixel_score[None], grad_in, grad_mid, grad_out_t.T, grad_gains)


def solution(mesh):
    placed = (
        P(("group", "sample"), "member", None, "tile", None),
        P(("group", "sample"), None, None, "tile"),
        P(("group", "sample"), None, "tile"),
        P(("group", "sample"), "member"),
        P(),
        P(),
        P(),
        P(),
    )
    return jax.shard_map(
        on_device,
        mesh=mesh,
        in_specs=placed,
        out_specs=(
            P(("group", "sample"), None, "member", "tile"),
            P("group", None),
            P("group", None),
            P("group", None),
            P("group", None),
        ),
        check_vma=False,
    )
```
